32 devices in a mesh: groups: 2 (over y), inst: 4 (over x, core), tp: 4 (over z).
Axes of the slice: x: 2, y: 2, z: 4, core: 2. Of those that a mesh axis runs over, the one named last changes fastest.
Arguments:
- hidden_rows: bfloat16 [128, 2, 8192], P(('groups', 'inst')), parts along dimension 0, may hold values from -6 to 6
- queries: bfloat16 [128, 2, 8192], P(('groups', 'inst'), None, 'tp'), parts along dimension 0
- key_pool: bfloat16 [384, 64, 1024], P(('groups', 'inst'), None, 'tp'), parts along dimension 0
- value_pool: bfloat16 [384, 64, 1024], P(('groups', 'inst'), None, 'tp'), parts along dimension 0, may hold values from -6 to 6
- page_table: int32 [128, 4], P(('groups', 'inst')), parts along dimension 0, may hold values from 0 to 47, as said below
- cache_length: int32 [128], P(('groups', 'inst')), parts along dimension 0, may hold values from 1 to 256, as said below
- new_owner: int32 [128, 1], P(('groups', 'inst')), parts along dimension 0, may hold values from 0 to 3; in each aligned block of 16 rows (0 to 15, 16 to 31, ...) at most 6 rows name the same one
- key_weight: bfloat16 [8192, 1024], P(None, 'tp'), may hold values from -0.0625 to 0.0625
- value_weight: bfloat16 [8192, 1024], P(None, 'tp'), may hold values from -0.0625 to 0.0625
Outputs:
- own_out: bfloat16 [128, 2, 8192], P(('groups', 'inst'), None, 'tp'), parts along dimension 0
- adopted_out: bfloat16 [8, 4, 24, 2, 2048], P(('groups', 'inst'), 'tp'), parts along dimension 0
- adopted_pool: bfloat16 [8, 4, 24, 2, 256, 256], P(('groups', 'inst'), 'tp'), parts along dimension 0
The draws below stay inside these ranges and needn't reach their ends.
There are 2 independent parts, one for each index of `groups`. The reference program is written for one: setup_inputs(seed, part) draws one part's arguments, and reference() takes and returns one part's arrays. A program takes and returns all parts, laid end to end along the dimension named above; an argument that names none is the same for every part. Nothing has to cross between parts.
Inputs may be any that keep to these rules, and one draw needn't show every extreme that they name: `page_table`: entries index blocks of the request's own instance pool; only the first ceil(cache_length / 64) entries of a row are read, and no block is read by two requests. `cache_length`: every instance has a request of exactly 256 tokens; each of its other requests needs at most 5/8 of 4 blocks, rounded down, and one of them needs exactly that many. `new_owner`: among the 16 requests of one instance at most 6 name the same instance, a bound that some block reaches of them.
All inputs are finite; a program needn't handle non-finite values.
Results may differ from the reference program's by a relative error of at most 0.0051.
Values may be sent and summed in bfloat16 or wider, within the bound.
No kernel may reach another device: no remote copies, remote signals or barrier semaphores. Data moves between devices by JAX's collectives and lax.ppermute only.
A program may use at most 128 MiB of HBM per device.

```python
import math
import jax
import jax.numpy as jnp
import numpy as np
from jax import lax

D = 8192
H = 64
KVH = 8
HD = 128
REQS = 16
BLK = 64
MAXP = 4
NB = 48
CAP = 6
ROWS = 64
N_INST = 4
N_TP = 4


def plan_requests(key):

    def per_instance(subkey):
        key_pages, key_longest, key_tail, key_order = jax.random.split(subkey, 4)
        request_index = jnp.arange(REQS)
        page_count = jax.random.randint(key_pages, (REQS,), 1, MAXP * 5 // 8 + 1)
        longest = jax.random.randint(key_longest, (), 0, REQS)
        second = (longest + 1) % REQS
        page_count = jnp.where(request_index == second, MAXP * 5 // 8, page_count)
        page_count = jnp.where(request_index == longest, MAXP, page_count)
        tail_tokens = jax.random.randint(key_tail, (REQS,), 1, BLK + 1)
        lengths = jnp.where(request_index == longest, MAXP * BLK, (page_count - 1) * BLK + tail_tokens)
        shuffled = jax.random.permutation(key_order, NB)
        offsets = jnp.cumsum(page_count) - page_count
        positions = (offsets[:, None] + jnp.arange(MAXP)[None, :]) % NB
        return (shuffled[positions].astype(jnp.int32), lengths.astype(jnp.int32))
    table, lengths = jax.vmap(per_instance)(jax.random.split(jax.random.fold_in(key, 11), N_INST))
    return (table.reshape(N_INST * REQS, MAXP), lengths.reshape(N_INST * REQS))


def draw_page_table(key, part):
    return plan_requests(key)[0]


def draw_cache_length(key, part):
    return plan_requests(key)[1]


def draw_queries(key, part):
    key = jax.random.fold_in(key, 3)
    full_shape = (N_INST * REQS, 2, H * HD)
    values_drawn = jax.random.normal(key, full_shape, jnp.float32)
    return values_drawn.astype(jnp.bfloat16)


def draw_key_pool(key, part):
    key = jax.random.fold_in(key, 5)
    full_shape = (N_INST * NB, BLK, KVH * HD)
    values_drawn = jax.random.normal(key, full_shape, jnp.float32)
    return values_drawn.astype(jnp.bfloat16)


def steps_of(key, dims, cuts, low, largest):
    loudness = 1.0
    for position, blocks in cuts:
        heights = jax.random.uniform(jax.random.fold_in(jax.random.fold_in(key, 6), position), (blocks,), jnp.float32, low / len(cuts), largest / len(cuts))
        loudness = loudness * jnp.repeat(jnp.exp(heights), dims[position] // blocks).reshape((-1,) + (1,) * (len(dims) - 1 - position))
    return loudness


def deal_out(rng, own, number, rows, number_of, top, reach, skew):
    ranking = jax.random.permutation(rng, number_of)
    heavy_load, common = portions_of(number_of, rows * top, reach, skew, True), portions_of(number_of, rows * top, reach, skew, False)
    places = jnp.arange(number_of)

    def named(tallies, turn):
        used = int((tallies > 0).sum())
        fixed = max(1, used // 4)
        moved = fixed + (places - fixed + turn * (used - fixed)) % max(1, number_of - fixed)
        return jnp.zeros((number_of,), jnp.int32).at[ranking[jnp.where(places < fixed, places, moved)]].set(jnp.asarray(tallies, jnp.int32))

    tallies = jnp.where(number % 4 == 0, named(heavy_load, number // 4), named(common, number - number // 4 - 1))
    mixed = jax.random.permutation(jax.random.fold_in(own, 3), number_of)
    giver, receiver = mixed[0:number_of // 2 * 2:2], mixed[1:number_of // 2 * 2:2]
    margin = jnp.minimum(tallies[giver] - 1, reach - tallies[receiver]) // 2
    margin = jnp.where((giver == ranking[0]) | (receiver == ranking[0]) | (tallies[receiver] == 0), 0, jnp.maximum(margin, 0))
    moved = jax.random.randint(jax.random.fold_in(own, 4), (number_of // 2,), 0, 1 << 20) % (margin + 1)
    tallies = tallies.at[giver].add(-moved).at[receiver].add(moved)
    labels = jnp.searchsorted(jnp.cumsum(tallies), jnp.arange(rows * top), side="right").astype(jnp.int32)
    grid = labels.reshape(top, rows).T
    grid = grid[jax.random.permutation(jax.random.fold_in(own, 1), rows)]
    turn = jax.random.randint(jax.random.fold_in(own, 2), (rows, 1), 0, top)
    return jnp.take_along_axis(grid, (jnp.arange(top)[None, :] + turn) % top, axis=1)


def portions_of(number_of, total, most, slope, full):
    weights = [(1 << 20) // math.isqrt(rank ** slope) + 1 for rank in range(1, number_of + 1)]
    largest = most if full else min(most, max(-(-total // number_of), total * weights[0] // sum(weights)))
    least = 1 if total - largest >= number_of - 1 else 0
    given, rest = [largest] + [least] * (number_of - 1), total - largest - least * (number_of - 1)
    while rest > 0:
        candidates = [i for i in range(1, number_of) if given[i] < largest] or [i for i in range(1, number_of) if given[i] < most]
        mass, left = sum([weights[i] for i in candidates]), rest
        for i in candidates:
            more = min(most - given[i], max(1, left * weights[i] // mass), rest)
            given[i] = given[i] + more
            rest = rest - more
    return np.array(given)


def normal_values(own_key, dims, deviation, bound, cuts=(), held_as=jnp.bfloat16):
    drawn = deviation * jax.random.normal(own_key, dims, jnp.float32)
    if cuts:
        drawn = drawn * steps_of(own_key, dims, cuts, -0.22, 0.18)
    return jnp.clip(drawn, -bound, bound).astype(held_as)


def setup_inputs(seed: int = 0, part: int = 0) -> dict:
    arg_keys = jax.random.split(jax.random.key(seed), 10)
    part_splits = jax.random.split(jax.random.fold_in(arg_keys[9], part), 10)
    hidden_rows = normal_values(part_splits[0], (ROWS, 2, D), 1.0, 6.0, ((0, 4),))
    queries = draw_queries(jax.random.fold_in(jax.random.fold_in(arg_keys[9], part), 71), part)
    key_pool = draw_key_pool(jax.random.fold_in(jax.random.fold_in(arg_keys[9], part), 71), part)
    value_pool = normal_values(part_splits[3], (N_INST * NB, BLK, KVH * HD), 1.0, 6.0, ((0, 4), (2, 4)))
    page_table = draw_page_table(jax.random.fold_in(jax.random.fold_in(arg_keys[9], part), 71), part)
    cache_length = draw_cache_length(jax.random.fold_in(jax.random.fold_in(arg_keys[9], part), 71), part)
    new_owner_keys = jax.random.split(jax.random.fold_in(part_splits[6], 1), ROWS // REQS)
    new_owner_turns = jax.random.permutation(jax.random.fold_in(part_splits[6], 3), ROWS // REQS)
    new_owner = jax.vmap(lambda own, number: deal_out(jax.random.fold_in(part_splits[6], 2), own, number, REQS, N_INST, 1, CAP, 2))(new_owner_keys, new_owner_turns).reshape((ROWS, 1))
    key_weight = normal_values(arg_keys[7], (D, KVH * HD), D ** -0.5, 0.0625, ((1, 4),))
    value_weight = normal_values(arg_keys[8], (D, KVH * HD), D ** -0.5, 0.0625, ((1, 4),))
    return dict(hidden_rows=hidden_rows, queries=queries, key_pool=key_pool, value_pool=value_pool, page_table=page_table, cache_length=cache_length, new_owner=new_owner, key_weight=key_weight, value_weight=value_weight)


ROTARY_BASE = 500000.0


def rotate(values, positions):
    head_width = values.shape[-1]
    half_width = head_width // 2
    frequency = ROTARY_BASE ** (-(jnp.arange(half_width, dtype=jnp.float32) * 2.0 / head_width))
    angles = positions[..., None, None] * frequency
    cosine = jnp.cos(angles)
    sine_part = jnp.sin(angles)
    first_half = values[..., :half_width]
    second_half = values[..., half_width:]
    return jnp.concatenate([first_half * cosine - second_half * sine_part, second_half * cosine + first_half * sine_part], axis=-1)


def new_tokens(hidden, weight_key, weight_value, lengths):
    count = hidden.shape[0]
    flat_rows = hidden.reshape(count * 2, hidden.shape[-1])
    raw_keys = jnp.dot(flat_rows, weight_key, preferred_element_type=jnp.float32).reshape(count, 2, -1, HD)
    positions = lengths.astype(jnp.float32)[:, None] + jnp.arange(2, dtype=jnp.float32)[None, :]
    fresh_keys = rotate(raw_keys, positions).reshape(count, 2, -1).astype(jnp.bfloat16)
    fresh_values = jnp.dot(flat_rows, weight_value, preferred_element_type=jnp.float32).reshape(count, 2, -1).astype(jnp.bfloat16)
    return fresh_keys, fresh_values


def attend(key_rows, value_rows, lengths, query_rows, fresh_keys, fresh_values):
    count = key_rows.shape[0]
    span_rows = key_rows.shape[1]
    head_groups = key_rows.shape[-1] // HD
    per_group = query_rows.shape[-1] // (head_groups * HD)
    query_heads = query_rows.reshape(count, 2, head_groups, per_group, HD).astype(jnp.float32)
    cache_keys = key_rows.reshape(count, span_rows, head_groups, HD).astype(jnp.float32)
    cache_values = value_rows.reshape(count, span_rows, head_groups, HD).astype(jnp.float32)
    new_keys = fresh_keys.reshape(count, 2, head_groups, HD).astype(jnp.float32)
    new_values = fresh_values.reshape(count, 2, head_groups, HD).astype(jnp.float32)
    scaling = HD ** -0.5
    cache_scores = jnp.einsum('sjgqe,stge->sjgqt', query_heads, cache_keys) * scaling
    live_mask = jnp.arange(span_rows)[None, :] < lengths[:, None]
    cache_scores = jnp.where(live_mask[:, None, None, None, :], cache_scores, -jnp.inf)
    fresh_scores = jnp.einsum('sjgqe,sige->sjgqi', query_heads, new_keys) * scaling
    allowed = jnp.arange(2)[None, :] <= jnp.arange(2)[:, None]
    fresh_scores = jnp.where(allowed[None, :, None, None, :], fresh_scores, -jnp.inf)
    highest = jnp.maximum(jnp.max(cache_scores, axis=-1), jnp.max(fresh_scores, axis=-1))
    cache_mass = jnp.exp(cache_scores - highest[..., None])
    fresh_mass = jnp.exp(fresh_scores - highest[..., None])
    total_mass = jnp.sum(cache_mass, axis=-1) + jnp.sum(fresh_mass, axis=-1)
    cache_weights = (cache_mass / total_mass[..., None]).astype(jnp.bfloat16).astype(jnp.float32)
    fresh_weights = (fresh_mass / total_mass[..., None]).astype(jnp.bfloat16).astype(jnp.float32)
    final_output = jnp.einsum('sjgqt,stge->sjgqe', cache_weights, cache_values) + jnp.einsum('sjgqi,sige->sjgqe', fresh_weights, new_values)
    return final_output.reshape(count, 2, -1).astype(jnp.bfloat16)


def reference(hidden_rows, queries, key_pool, value_pool, page_table, cache_length, new_owner, key_weight, value_weight):
    def per_instance(pieces):
        hidden, query_rows, pool_keys, pool_values, pages, lengths = pieces
        key_rows = pool_keys[pages].reshape(REQS, MAXP * BLK, -1)
        value_rows = pool_values[pages].reshape(REQS, MAXP * BLK, -1)
        fresh_keys, fresh_values = new_tokens(hidden, key_weight, value_weight, lengths)
        return attend(key_rows, value_rows, lengths, query_rows, fresh_keys, fresh_values)

    attended = lax.map(per_instance, (
        hidden_rows.reshape(N_INST, REQS, 2, D),
        queries.reshape(N_INST, REQS, 2, H * HD),
        key_pool.reshape(N_INST, NB, BLK, KVH * HD),
        value_pool.reshape(N_INST, NB, BLK, KVH * HD),
        page_table.reshape(N_INST, REQS, MAXP),
        cache_length.reshape(N_INST, REQS)))
    group_width = H * HD // N_TP
    keep_group = jnp.arange(N_TP) < N_TP // 2
    split_cols = attended.reshape(N_INST * REQS, 2, N_TP, group_width)
    own_out = jnp.where(keep_group[None, None, :, None], split_cols, jnp.zeros_like(split_cols)).reshape(N_INST * REQS, 2, H * HD)
    owner_ids = new_owner[:, 0].reshape(N_INST, REQS)
    request_index = jnp.arange(REQS)
    same_owner = owner_ids[:, :, None] == owner_ids[:, None, :]
    earlier = request_index[None, :] < request_index[:, None]
    arrival = jnp.sum(same_owner & earlier[None, :, :], axis=2)
    slot_of = jnp.arange(N_INST)[:, None] * CAP + arrival
    placing = (owner_ids[None, None, :, :] == jnp.arange(N_INST)[:, None, None, None]) & (slot_of[None, None, :, :] == jnp.arange(N_INST * CAP)[None, :, None, None])
    gathered = jnp.einsum('dxpr,prjc->dxjc', placing.astype(jnp.float32), attended.astype(jnp.float32), precision=lax.Precision.HIGHEST).astype(jnp.bfloat16)
    gathered = gathered.reshape(N_INST, N_INST * CAP, 2, N_TP, group_width)
    moved_part = gathered[:, :, :, N_TP // 2:, :]
    adopted_out = jnp.concatenate([moved_part, jnp.zeros_like(moved_part)], axis=3).transpose(0, 3, 1, 2, 4)

    pool_width = KVH * HD // N_TP
    half_count = N_TP // 2
    span_rows = MAXP * BLK
    source_request = jnp.sum(jnp.where(placing, request_index[None, None, None, :], 0), axis=(2, 3)).astype(jnp.int32)
    filled = jnp.any(placing, axis=(2, 3))
    source_instance = (jnp.arange(N_INST * CAP) // CAP).astype(jnp.int32)
    lengths_all = cache_length.reshape(N_INST, REQS)
    pages_all = page_table.reshape(N_INST, REQS, MAXP)
    key_released = key_pool.reshape(N_INST, NB, BLK, N_TP, pool_width)[:, :, :, half_count:, :]
    value_released = value_pool.reshape(N_INST, NB, BLK, N_TP, pool_width)[:, :, :, half_count:, :]

    def per_owner(pieces):
        rows_taken, used = pieces
        slot_len = jnp.where(used, lengths_all[source_instance, rows_taken], 0)
        page_ids = pages_all[source_instance, rows_taken]
        keys_now = key_released[source_instance[:, None], page_ids].reshape(N_INST * CAP, span_rows, half_count, pool_width)
        values_now = value_released[source_instance[:, None], page_ids].reshape(N_INST * CAP, span_rows, half_count, pool_width)
        live = (jnp.arange(span_rows)[None, :] < slot_len[:, None])[:, :, None, None]
        keys_now = jnp.where(live, keys_now, jnp.zeros_like(keys_now))
        values_now = jnp.where(live, values_now, jnp.zeros_like(values_now))
        both = jnp.stack([keys_now, values_now], axis=1).transpose(3, 0, 1, 2, 4)
        return jnp.concatenate([both, jnp.zeros_like(both)], axis=0)

    adopted_pool = lax.map(per_owner, (source_request, filled))
    return own_out, adopted_out, adopted_pool
```

```python
import functools

import jax
import jax.numpy as jnp
from jax import lax
from jax.experimental import pallas as pl
from jax.experimental.pallas import tpu as pltpu
from jax.sharding import PartitionSpec as P

HD = 128
ROTARY_BASE = 500000.0
UNIT = 16
ANY = pl.BlockSpec(memory_space=pl.ANY)


def rotate(values, positions):
    head_width = values.shape[-1]
    half_width = head_width // 2
    frequency = ROTARY_BASE ** (-(jnp.arange(half_width, dtype=jnp.float32) * 2.0 / head_width))
    angles = positions[..., None, None] * frequency
    cosine = jnp.cos(angles)
    sine_part = jnp.sin(angles)
    first_half = values[..., :half_width]
    second_half = values[..., half_width:]
    return jnp.concatenate(
        [
            first_half * cosine - second_half * sine_part,
            second_half * cosine + first_half * sine_part,
        ],
        axis=-1,
    )


def new_tokens(hidden, weight_key, weight_value, lengths):
    count = hidden.shape[0]
    flat_rows = hidden.reshape(count * 2, hidden.shape[-1])
    raw_keys = jnp.dot(flat_rows, weight_key, preferred_element_type=jnp.float32).reshape(
        count, 2, -1, HD
    )
    positions = lengths.astype(jnp.float32)[:, None] + jnp.arange(2, dtype=jnp.float32)[None, :]
    fresh_keys = rotate(raw_keys, positions).reshape(count, 2, -1).astype(jnp.bfloat16)
    fresh_values = (
        jnp.dot(flat_rows, weight_value, preferred_element_type=jnp.float32)
        .reshape(count, 2, -1)
        .astype(jnp.bfloat16)
    )
    return (fresh_keys, fresh_values)


def attend(key_rows, value_rows, lengths, query_rows, fresh_keys, fresh_values):
    count = key_rows.shape[0]
    span_rows = key_rows.shape[1]
    head_groups = key_rows.shape[-1] // HD
    per_group = query_rows.shape[-1] // (head_groups * HD)
    query_heads = query_rows.reshape(count, 2, head_groups, per_group, HD)
    cache_keys = key_rows.reshape(count, span_rows, head_groups, HD)
    cache_values = value_rows.reshape(count, span_rows, head_groups, HD)
    new_keys = fresh_keys.reshape(count, 2, head_groups, HD)
    new_values = fresh_values.reshape(count, 2, head_groups, HD)
    scaling = HD ** (-0.5)
    cache_scores = (
        jnp.einsum("sjgqe,stge->sjgqt", query_heads, cache_keys, preferred_element_type=jnp.float32)
        * scaling
    )
    live_mask = jnp.arange(span_rows)[None, :] < lengths[:, None]
    cache_scores = jnp.where(live_mask[:, None, None, None, :], cache_scores, -jnp.inf)
    fresh_scores = (
        jnp.einsum("sjgqe,sige->sjgqi", query_heads, new_keys, preferred_element_type=jnp.float32)
        * scaling
    )
    allowed = jnp.arange(2)[None, :] <= jnp.arange(2)[:, None]
    fresh_scores = jnp.where(allowed[None, :, None, None, :], fresh_scores, -jnp.inf)
    highest = jnp.maximum(jnp.max(cache_scores, axis=-1), jnp.max(fresh_scores, axis=-1))
    cache_mass = jnp.exp(cache_scores - highest[..., None])
    fresh_mass = jnp.exp(fresh_scores - highest[..., None])
    total_mass = jnp.sum(cache_mass, axis=-1) + jnp.sum(fresh_mass, axis=-1)
    cache_weights = (cache_mass / total_mass[..., None]).astype(jnp.bfloat16)
    fresh_weights = (fresh_mass / total_mass[..., None]).astype(jnp.bfloat16)
    final_output = jnp.einsum(
        "sjgqt,stge->sjgqe", cache_weights, cache_values, preferred_element_type=jnp.float32
    )
    final_output = final_output + jnp.einsum(
        "sjgqi,sige->sjgqe", fresh_weights, new_values, preferred_element_type=jnp.float32
    )
    return final_output.reshape(count, 2, -1).astype(jnp.bfloat16)


def padded(lengths):
    return (lengths + (UNIT - 1)) // UNIT * UNIT


def pack_kernel(table, lens, keys, values, first, second, pile, sems):
    block = keys.shape[1]
    row = lax.broadcasted_iota(jnp.int32, (block, keys.shape[2]), 0)
    cut = first.shape[1]

    def request(r, start):
        live = lens[r]
        for page in range(table.shape[1]):
            left = live - page * block

            @pl.when(left > 0)
            def _():
                source = table[r, page]
                place = pl.ds(pl.multiple_of(start + page * block, UNIT), block)
                mask = row < left
                for index, pool in enumerate((keys, values)):
                    kept = pool[source]
                    pile[index, place, :] = jnp.where(mask, kept, jnp.zeros_like(kept))

        return start + padded(live)

    lax.fori_loop(0, lens.shape[0], request, jnp.int32(0))
    copies = [
        pltpu.make_async_copy(pile.at[:, pl.ds(0, cut), :], first, sems.at[0]),
        pltpu.make_async_copy(pile.at[:, pl.ds(cut, second.shape[1]), :], second, sems.at[1]),
    ]
    for copy in copies:
        copy.start()
    for copy in copies:
        copy.wait()


def pack(page_table, lengths, key_pool, value_pool, most, cut):
    block, width = key_pool.shape[1:]
    return pl.pallas_call(
        pack_kernel,
        out_shape=(
            jax.ShapeDtypeStruct((2, cut, width), jnp.bfloat16),
            jax.ShapeDtypeStruct((2, most - cut, width), jnp.bfloat16),
        ),
        grid_spec=pltpu.PrefetchScalarGridSpec(
            num_scalar_prefetch=2,
            grid=(1,),
            in_specs=[pl.BlockSpec(key_pool.shape, lambda i, *_: (0, 0, 0))] * 2,
            out_specs=[ANY, ANY],
            scratch_shapes=[
                pltpu.VMEM((2, most + block, width), jnp.bfloat16),
                pltpu.SemaphoreType.DMA((2,)),
            ],
        ),
        compiler_params=pltpu.CompilerParams(vmem_limit_bytes=32 * 1024 * 1024),
        name="pack",
    )(page_table, lengths, key_pool, value_pool)


def unpack_kernel(low, high, capacity, blocks, starts, sizes, *refs):
    count = len(refs) - 5
    piles, out, stage, inward, outward = refs[:count], refs[-4], refs[-3], refs[-2], refs[-1]

    def span(j, c):
        start, size = starts[j, c], sizes[j, c]
        begin = jnp.maximum(start, low)
        rows = jnp.minimum(start + size, high) - begin
        slot = blocks[j] * capacity + c
        return start, begin, rows, slot

    def arriving(j, c):
        _, begin, rows, slot = span(j, c)
        rows = pl.multiple_of(rows, UNIT)
        return pltpu.make_async_copy(
            piles[j].at[:, pl.ds(pl.multiple_of(begin - low, UNIT), rows), :],
            stage.at[j * capacity + c, :, pl.ds(0, rows), :],
            inward.at[j * capacity + c],
        )

    def leaving(j, c):
        start, begin, rows, slot = span(j, c)
        rows = pl.multiple_of(rows, UNIT)
        return pltpu.make_async_copy(
            stage.at[j * capacity + c, :, pl.ds(0, rows), :],
            out.at[slot, :, pl.ds(pl.multiple_of(begin - start, UNIT), rows), :],
            outward.at[j * capacity + c],
        )

    def each(action):
        for j in range(count):
            for c in range(capacity):
                rows = span(j, c)[2]

                @pl.when(rows > 0)
                def _():
                    action(j, c)

    def turn(j, c):
        arriving(j, c).wait()
        leaving(j, c).start()

    each(lambda j, c: arriving(j, c).start())
    each(turn)
    each(lambda j, c: leaving(j, c).wait())


def unpack(plan, piles, out, low, high):
    blocks, starts, sizes = plan[0], plan[1], plan[2]
    capacity = starts.shape[1]
    count = len(piles)
    return pl.pallas_call(
        functools.partial(unpack_kernel, low, high, capacity),
        out_shape=jax.ShapeDtypeStruct(out.shape, out.dtype),
        grid_spec=pltpu.PrefetchScalarGridSpec(
            num_scalar_prefetch=3,
            grid=(),
            in_specs=[ANY] * (count + 1),
            out_specs=ANY,
            scratch_shapes=[
                pltpu.VMEM((count * capacity,) + out.shape[1:], out.dtype),
                pltpu.SemaphoreType.DMA((count * capacity,)),
                pltpu.SemaphoreType.DMA((count * capacity,)),
            ],
        ),
        input_output_aliases={3 + count: 0},
        compiler_params=pltpu.CompilerParams(vmem_limit_bytes=32 * 1024 * 1024),
        name="unpack",
    )(blocks, starts, sizes, *piles, out)


def place(plan, sources, slots):
    blocks, sizes, rows = plan[0], plan[2], plan[3]
    capacity = sizes.shape[1]
    shape = (slots,) + sources[0].shape[1:]

    def body(blocks, sizes, rows, *refs):
        out = refs[-1]
        out[...] = jnp.zeros_like(out)
        for j in range(len(sources)):
            for c in range(capacity):

                @pl.when(sizes[j, c] > 0)
                def _():
                    out[blocks[j] * capacity + c] = refs[j][rows[j, c]]

    return pl.pallas_call(
        body,
        out_shape=jax.ShapeDtypeStruct(shape, jnp.bfloat16),
        grid_spec=pltpu.PrefetchScalarGridSpec(
            num_scalar_prefetch=3,
            grid=(1,),
            in_specs=[pl.BlockSpec(sources[0].shape, lambda i, *_: (0, 0, 0))] * len(sources),
            out_specs=pl.BlockSpec(shape, lambda i, *_: (0, 0, 0)),
        ),
        compiler_params=pltpu.CompilerParams(vmem_limit_bytes=32 * 1024 * 1024),
        name="place",
    )(blocks, sizes, rows, *sources)


def strides(count):
    bits = []
    step = count // 2
    while step:
        bits.append(step)
        step //= 2
    return bits


def local(
    hidden_rows,
    queries,
    key_pool,
    value_pool,
    page_table,
    cache_length,
    new_owner,
    key_weight,
    value_weight,
):
    tp = lax.axis_size("tp")
    halved_count = tp // 2
    remaining_device = lax.axis_index("tp") < halved_count
    instances = lax.axis_size("inst")
    groups = lax.axis_size("groups")
    me = lax.axis_index("inst")
    requests = cache_length.shape[0]
    pages_most = page_table.shape[1]
    block_rows = key_pool.shape[1]
    group_width = key_pool.shape[2]
    capacity = max(2, 3 * requests // (2 * instances))
    slot_count = instances * capacity
    span_rows = pages_most * block_rows
    most = span_rows + (requests - 1) * (pages_most * 5 // 8) * block_rows
    step = block_rows
    cut = min(most, 12 * block_rows)

    def down(value):
        return lax.ppermute(value, "tp", [(t + halved_count, t) for t in range(halved_count)])

    def across(value, stride):
        pairs = [
            (i * tp + t, (i ^ stride) * tp + t)
            for i in range(instances)
            for t in range(halved_count)
        ]
        return lax.ppermute(value, ("inst", "tp"), pairs)

    def spread(value):
        parts = [value]
        for stride in strides(instances):
            parts = parts + [across(part, stride) for part in parts]
        return parts

    first, second = pack(page_table, cache_length, key_pool, value_pool, most, cut)
    head = down(first)

    facts = jnp.stack([cache_length, new_owner[:, 0]])[None]
    order = [0]
    for stride in strides(instances):
        facts = jnp.concatenate(
            [facts, lax.ppermute(facts, "inst", [(i, i ^ stride) for i in range(instances)])]
        )
        order = order + [o ^ stride for o in order]
    sizes_all = padded(facts[:, 0])
    longest = jnp.max(jnp.sum(sizes_all, axis=1))
    for stride in strides(groups):
        longest = jnp.maximum(
            longest,
            lax.ppermute(longest[None], "groups", [(g, g ^ stride) for g in range(groups)])[0],
        )
    mine = (facts[:, 1] == me) & remaining_device
    earlier = jnp.arange(requests)[None, :] < jnp.arange(requests)[:, None]
    starts_all = jnp.sum(jnp.where(earlier[None], sizes_all[:, None, :], 0), axis=2)
    rank = jnp.sum(jnp.where(earlier[None], mine[:, None, :].astype(jnp.int32), 0), axis=2)
    chosen = mine[:, None, :] & (rank[:, None, :] == jnp.arange(capacity)[None, :, None])

    def chosen_of(values):
        return jnp.sum(jnp.where(chosen, values, 0), axis=2)

    plan = (
        me ^ jnp.array(order, jnp.int32),
        chosen_of(starts_all[:, None, :]),
        chosen_of(sizes_all[:, None, :]),
        chosen_of(jnp.arange(requests)[None, None, :]),
    )

    own_keys = key_pool[page_table].reshape(requests, span_rows, group_width)
    own_values = value_pool[page_table].reshape(requests, span_rows, group_width)
    own_fresh_k, own_fresh_v = new_tokens(hidden_rows, key_weight, value_weight, cache_length)
    local_output = attend(own_keys, own_values, cache_length, queries, own_fresh_k, own_fresh_v)

    def finish(more, head, second, attended, plan):
        pool = jnp.zeros((slot_count, 2, span_rows, group_width), jnp.bfloat16)
        last = min(more, 2 * block_rows)
        pieces = []
        if more > last:
            pieces.append((0, more - last))
        if more:
            pieces.append((more - last, more))
        arrived = [(down(second[:, a:b]), a, b) for a, b in pieces]
        rows = down(attended)
        pool = unpack(plan, spread(head), pool, 0, cut)
        for piece, a, b in arrived:
            pool = unpack(plan, spread(piece), pool, cut + a, cut + b)
        return place(plan, spread(rows), slot_count), pool

    branches = [
        functools.partial(finish, more) for more in range(0, most - cut + 1, step)
    ]
    choice = jnp.clip((longest - cut + step - 1) // step, 0, len(branches) - 1)
    inherited, kept_cache = lax.switch(choice, branches, head, second, local_output, plan)
    local_output = jnp.where(remaining_device, local_output, jnp.zeros_like(local_output))
    return (local_output, inherited[None, None], kept_cache[None, None])


def solution(mesh):
    placed = (
        P(("groups", "inst"), None, None),
        P(("groups", "inst"), None, "tp"),
        P(("groups", "inst"), None, "tp"),
        P(("groups", "inst"), None, "tp"),
        P(("groups", "inst"), None),
        P(("groups", "inst")),
        P(("groups", "inst"), None),
        P(None, "tp"),
        P(None, "tp"),
    )
    return jax.shard_map(
        local,
        mesh=mesh,
        in_specs=placed,
        out_specs=(
            P(("groups", "inst"), None, "tp"),
            P(("groups", "inst"), "tp", None, None, None),
            P(("groups", "inst"), "tp", None, None, None, None),
        ),
        check_vma=False,
    )
```

```python
import functools

import jax
import jax.numpy as jnp
from jax import lax
from jax.experimental import pallas as pl
from jax.experimental.pallas import tpu as pltpu
from jax.sharding import PartitionSpec as P

HD = 128
ROTARY_BASE = 500000.0
UNIT = 16
FIRST, STEP = 18, 2
ANY = pl.BlockSpec(memory_space=pl.ANY)
HBM = pl.BlockSpec(memory_space=pltpu.HBM)
VMEM_LIMIT = 60 * 1024 * 1024


def rotate(values, positions):
    head_width = values.shape[-1]
    half_width = head_width // 2
    frequency = ROTARY_BASE ** (-(jnp.arange(half_width, dtype=jnp.float32) * 2.0 / head_width))
    angles = positions[..., None, None] * frequency
    cosine = jnp.cos(angles)
    sine_part = jnp.sin(angles)
    first_half = values[..., :half_width]
    second_half = values[..., half_width:]
    return jnp.concatenate(
        [
            first_half * cosine - second_half * sine_part,
            second_half * cosine + first_half * sine_part,
        ],
        axis=-1,
    )


def new_tokens(hidden, weight_key, weight_value, lengths):
    count = hidden.shape[0]
    flat_rows = hidden.reshape(count * 2, hidden.shape[-1])
    raw_keys = lax.optimization_barrier(
        jnp.dot(flat_rows, weight_key, preferred_element_type=jnp.float32)
    ).reshape(count, 2, -1, HD)
    positions = lengths.astype(jnp.float32)[:, None] + jnp.arange(2, dtype=jnp.float32)[None, :]
    fresh_keys = rotate(raw_keys, positions).reshape(count, 2, -1).astype(jnp.bfloat16)
    fresh_values = (
        jnp.dot(flat_rows, weight_value, preferred_element_type=jnp.float32)
        .reshape(count, 2, -1)
        .astype(jnp.bfloat16)
    )
    return (fresh_keys, fresh_values)


def attend(key_rows, value_rows, lengths, query_rows, fresh_keys, fresh_values):
    count = key_rows.shape[0]
    span_rows = key_rows.shape[1]
    head_groups = key_rows.shape[-1] // HD
    per_group = query_rows.shape[-1] // (head_groups * HD)
    query_heads = query_rows.reshape(count, 2, head_groups, per_group, HD)
    cache_keys = key_rows.reshape(count, span_rows, head_groups, HD)
    cache_values = value_rows.reshape(count, span_rows, head_groups, HD)
    new_keys = fresh_keys.reshape(count, 2, head_groups, HD)
    new_values = fresh_values.reshape(count, 2, head_groups, HD)
    scaling = HD ** (-0.5)
    cache_scores = (
        jnp.einsum("sjgqe,stge->sjgqt", query_heads, cache_keys, preferred_element_type=jnp.float32)
        * scaling
    )
    live_mask = jnp.arange(span_rows)[None, :] < lengths[:, None]
    cache_scores = jnp.where(live_mask[:, None, None, None, :], cache_scores, -jnp.inf)
    fresh_scores = (
        jnp.einsum("sjgqe,sige->sjgqi", query_heads, new_keys, preferred_element_type=jnp.float32)
        * scaling
    )
    allowed = jnp.arange(2)[None, :] <= jnp.arange(2)[:, None]
    fresh_scores = jnp.where(allowed[None, :, None, None, :], fresh_scores, -jnp.inf)
    highest = jnp.maximum(jnp.max(cache_scores, axis=-1), jnp.max(fresh_scores, axis=-1))
    cache_mass = jnp.exp(cache_scores - highest[..., None])
    fresh_mass = jnp.exp(fresh_scores - highest[..., None])
    total_mass = jnp.sum(cache_mass, axis=-1) + jnp.sum(fresh_mass, axis=-1)
    cache_weights = (cache_mass / total_mass[..., None]).astype(jnp.bfloat16)
    fresh_weights = (fresh_mass / total_mass[..., None]).astype(jnp.bfloat16)
    final_output = jnp.einsum(
        "sjgqt,stge->sjgqe", cache_weights, cache_values, preferred_element_type=jnp.float32
    )
    final_output = final_output + jnp.einsum(
        "sjgqi,sige->sjgqe", fresh_weights, new_values, preferred_element_type=jnp.float32
    )
    return final_output.reshape(count, 2, -1).astype(jnp.bfloat16)


def padded(lengths):
    return (lengths + (UNIT - 1)) // UNIT * UNIT


def strides(count):
    bits = []
    step = count // 2
    while step:
        bits.append(step)
        step //= 2
    return bits


def nearness(apart, steps):
    return sum((apart < step).astype(jnp.int32) for step in steps)


def pack_kernel(cuts, steps, table, lens, owners, keys, values, *refs):
    parts = refs[: len(cuts)]
    pools, pile, arrived, left_sems = refs[len(cuts) :]
    count, pages_most = lens.shape[0], table.shape[0]
    block = keys.shape[1]
    row = lax.broadcasted_iota(jnp.int32, (UNIT, keys.shape[2]), 0)
    me = lax.axis_index("inst")
    loads = [
        pltpu.make_async_copy(pool, pools.at[index], arrived.at[index])
        for index, pool in enumerate((keys, values))
    ]
    for load in loads:
        load.start()
    for load in loads:
        load.wait()

    def turn(i, start):
        r = lax.rem(i, count)
        live = lens[r]
        here = nearness(jnp.bitwise_xor(owners[r], me), steps) == i // count

        @pl.when(here)
        def _():
            for page in range(pages_most):

                @pl.when(live > page * block)
                def _():
                    source = table[page, r]
                    place = pl.ds(pl.multiple_of(start + page * block, UNIT), block)
                    for index in range(2):
                        pile[index, place, :] = pools[index, source]

            ending = padded(live) - UNIT
            place = pl.ds(pl.multiple_of(start + ending, UNIT), UNIT)
            mask = row < live - ending
            for index in range(2):
                kept = pile[index, place, :]
                pile[index, place, :] = jnp.where(mask, kept, jnp.zeros_like(kept))

        return start + jnp.where(here, padded(live), 0)

    lax.fori_loop(0, count * (len(steps) + 1), turn, jnp.int32(0))
    leaving = [
        pltpu.make_async_copy(
            pile.at[:, pl.ds(low, high - low), :], parts[number], left_sems.at[number]
        )
        for number, (low, high) in enumerate(cuts)
    ]
    for copy in leaving:
        copy.start()
    for copy in leaving:
        copy.wait()


def pack(page_table, lengths, owners, key_pool, value_pool, cuts, steps):
    width = key_pool.shape[2]
    block = key_pool.shape[1]
    return pl.pallas_call(
        functools.partial(pack_kernel, cuts, steps),
        out_shape=tuple(
            jax.ShapeDtypeStruct((2, high - low, width), jnp.bfloat16) for low, high in cuts
        ),
        grid_spec=pltpu.PrefetchScalarGridSpec(
            num_scalar_prefetch=3,
            grid=(),
            in_specs=[HBM, HBM],
            out_specs=[HBM] * len(cuts),
            scratch_shapes=[
                pltpu.VMEM((2,) + key_pool.shape, jnp.bfloat16),
                pltpu.VMEM((2, cuts[-1][1] + block, width), jnp.bfloat16),
                pltpu.SemaphoreType.DMA((2,)),
                pltpu.SemaphoreType.DMA((len(cuts),)),
            ],
        ),
        compiler_params=pltpu.CompilerParams(vmem_limit_bytes=VMEM_LIMIT),
        name="pack",
    )(page_table.T, lengths, owners, key_pool, value_pool)


def prepare_kernel(count, pile, *refs):
    parts, pool = refs[:count], refs[count]
    held, blank, arrived, sems, pool_sems = refs[count + 1 :]
    load = pltpu.make_async_copy(pile, held, arrived)
    load.start()
    blank[...] = jnp.zeros_like(blank)
    copies = [
        pltpu.make_async_copy(blank, pool.at[slot], pool_sems.at[slot])
        for slot in range(pool.shape[0])
    ]
    for copy in copies:
        copy.start()
    load.wait()
    copies += [
        pltpu.make_async_copy(held.at[:, pl.ds(0, part.shape[1]), :], part, sems.at[number])
        for number, part in enumerate(parts)
    ]
    for copy in copies[pool.shape[0] :]:
        copy.start()
    for copy in copies:
        copy.wait()


def prepare(pile, sizes, pool_shape):
    *parts, pool = pl.pallas_call(
        functools.partial(prepare_kernel, len(sizes)),
        out_shape=[
            jax.ShapeDtypeStruct((2, size, pile.shape[2]), pile.dtype) for size in sizes
        ]
        + [jax.ShapeDtypeStruct(pool_shape, pile.dtype)],
        in_specs=[HBM],
        out_specs=[HBM] * (len(sizes) + 1),
        scratch_shapes=[
            pltpu.VMEM(pile.shape, pile.dtype),
            pltpu.VMEM(pool_shape[1:], pile.dtype),
            pltpu.SemaphoreType.DMA,
            pltpu.SemaphoreType.DMA((len(sizes),)),
            pltpu.SemaphoreType.DMA((pool_shape[0],)),
        ],
        compiler_params=pltpu.CompilerParams(vmem_limit_bytes=VMEM_LIMIT),
        name="prepare",
    )(pile)
    return parts, pool


def entry(plan, count, capacity, kind, j, c):
    return plan[count + (kind * count + j) * capacity + c]


def unpack_kernel(low, high, total, capacity, numbers, plan, *refs):
    count = len(numbers)
    piles, out, stage, inward, outward = refs[:count], refs[-4], refs[-3], refs[-2], refs[-1]

    def span(j, c):
        start = entry(plan, total, capacity, 0, j, c)
        begin = jnp.maximum(start, low)
        end = jnp.minimum(start + entry(plan, total, capacity, 1, j, c), high)
        return start, begin, end - begin

    def arriving(k, c):
        _, begin, rows = span(numbers[k], c)
        rows = pl.multiple_of(rows, UNIT)
        return pltpu.make_async_copy(
            piles[k].at[:, pl.ds(pl.multiple_of(begin - low, UNIT), rows), :],
            stage.at[k * capacity + c, :, pl.ds(0, rows), :],
            inward.at[k * capacity + c],
        )

    def leaving(k, c):
        start, begin, rows = span(numbers[k], c)
        rows = pl.multiple_of(rows, UNIT)
        return pltpu.make_async_copy(
            stage.at[k * capacity + c, :, pl.ds(0, rows), :],
            out.at[
                plan[numbers[k]] * capacity + c,
                :,
                pl.ds(pl.multiple_of(begin - start, UNIT), rows),
                :,
            ],
            outward.at[k * capacity + c],
        )

    def each(action):
        for k in range(count):

            def slot(c, carry):
                @pl.when(span(numbers[k], c)[2] > 0)
                def _():
                    action(k, c)

                return carry

            lax.fori_loop(0, capacity, slot, 0)

    def turn(k, c):
        arriving(k, c).wait()
        leaving(k, c).start()

    each(lambda k, c: arriving(k, c).start())
    each(turn)
    each(lambda k, c: leaving(k, c).wait())


def unpack(plan, total, capacity, parts, out, low, high):
    count = len(parts)
    numbers = [number for _, number in parts]
    return pl.pallas_call(
        functools.partial(unpack_kernel, low, high, total, capacity, numbers),
        out_shape=jax.ShapeDtypeStruct(out.shape, out.dtype),
        grid_spec=pltpu.PrefetchScalarGridSpec(
            num_scalar_prefetch=1,
            grid=(),
            in_specs=[ANY] * count + [HBM],
            out_specs=HBM,
            scratch_shapes=[
                pltpu.VMEM((count * capacity,) + out.shape[1:], out.dtype),
                pltpu.SemaphoreType.DMA((count * capacity,)),
                pltpu.SemaphoreType.DMA((count * capacity,)),
            ],
        ),
        input_output_aliases={1 + count: 0},
        compiler_params=pltpu.CompilerParams(vmem_limit_bytes=VMEM_LIMIT),
        name="unpack",
    )(plan, *[pile for pile, _ in parts], out)


def place_kernel(total, capacity, numbers, plan, *refs):
    out = refs[-1]
    out[...] = jnp.zeros_like(out)
    for k, j in enumerate(numbers):

        def slot(c, carry):
            r = entry(plan, total, capacity, 2, j, c)

            @pl.when(r >= 0)
            def _():
                out[plan[j] * capacity + c] = refs[k][r]

            return carry

        lax.fori_loop(0, capacity, slot, 0)


def place(plan, total, capacity, parts):
    source = parts[0][0].shape
    shape = (total * capacity,) + source[1:]
    return pl.pallas_call(
        functools.partial(place_kernel, total, capacity, [number for _, number in parts]),
        out_shape=jax.ShapeDtypeStruct(shape, jnp.bfloat16),
        grid_spec=pltpu.PrefetchScalarGridSpec(
            num_scalar_prefetch=1,
            grid=(1,),
            in_specs=[pl.BlockSpec(source, lambda i, *_: (0, 0, 0))] * len(parts),
            out_specs=pl.BlockSpec(shape, lambda i, *_: (0, 0, 0)),
        ),
        compiler_params=pltpu.CompilerParams(vmem_limit_bytes=VMEM_LIMIT),
        name="place",
    )(plan, *[part for part, _ in parts])


def local(
    hidden_rows,
    queries,
    key_pool,
    value_pool,
    page_table,
    cache_length,
    new_owner,
    key_weight,
    value_weight,
):
    tp = lax.axis_size("tp")
    halved_count = tp // 2
    remaining_device = lax.axis_index("tp") < halved_count
    instances = lax.axis_size("inst")
    groups = lax.axis_size("groups")
    me = lax.axis_index("inst")
    requests = cache_length.shape[0]
    pages_most = page_table.shape[1]
    block_rows = key_pool.shape[1]
    group_width = key_pool.shape[2]
    capacity = max(2, 3 * requests // (2 * instances))
    slot_count = instances * capacity
    span_rows = pages_most * block_rows
    most = span_rows + (requests - 1) * (pages_most * 5 // 8) * block_rows
    step = STEP * block_rows
    cut = min(most, FIRST * block_rows)
    all_steps = strides(instances)
    order = [0]
    for stride in all_steps:
        order = order + [o ^ stride for o in order]

    def down(value):
        return lax.ppermute(value, "tp", [(t + halved_count, t) for t in range(halved_count)])

    def across(value, stride, low):
        pairs = [
            (i * tp + t, (i ^ stride) * tp + t)
            for i in range(instances)
            for t in range(low, low + halved_count)
        ]
        return lax.ppermute(value, ("inst", "tp"), pairs)

    def spread(value, steps, low=0):
        parts = [(value, 0)]
        for stride in steps:
            parts = parts + [(across(part, stride, low), o ^ stride) for part, o in parts]
        return [(part, order.index(o)) for part, o in parts]

    first, rest = pack(
        page_table,
        cache_length,
        new_owner[:, 0],
        key_pool,
        value_pool,
        [(0, cut), (cut, most)],
        all_steps,
    )
    sample = down(first[:1, :UNIT, :HD])
    first = down(first)
    _, rest, hidden_rows, lengths, new_owner, page_table = lax.optimization_barrier(
        (sample, rest, hidden_rows, cache_length, new_owner, page_table)
    )
    own_keys = key_pool[page_table].reshape(requests, span_rows, group_width)
    own_values = value_pool[page_table].reshape(requests, span_rows, group_width)
    own_fresh_k, own_fresh_v = new_tokens(hidden_rows, key_weight, value_weight, lengths)

    facts = jnp.stack([lengths, new_owner[:, 0]])[None]
    for stride in all_steps:
        facts = jnp.concatenate(
            [facts, lax.ppermute(facts, "inst", [(i, i ^ stride) for i in range(instances)])]
        )
    sources = me ^ jnp.array(order, jnp.int32)
    sizes_all = padded(facts[:, 0])
    near = nearness(facts[:, 1] ^ sources[:, None], all_steps)
    extents = jnp.stack(
        [
            jnp.max(jnp.sum(sizes_all, axis=1)),
            jnp.max(jnp.sum(jnp.where(near == 0, sizes_all, 0), axis=1)),
        ]
    )
    for stride in strides(groups):
        extents = jnp.maximum(
            extents,
            lax.ppermute(extents, "groups", [(g, g ^ stride) for g in range(groups)]),
        )
    mine = facts[:, 1] == me
    index = jnp.arange(requests)
    earlier = index[None, :] < index[:, None]
    packed_earlier = (near[:, None, :] < near[:, :, None]) | (
        (near[:, None, :] == near[:, :, None]) & earlier[None]
    )
    starts_all = jnp.sum(jnp.where(packed_earlier, sizes_all[:, None, :], 0), axis=2)
    rank = jnp.sum(jnp.where(earlier[None], mine[:, None, :].astype(jnp.int32), 0), axis=2)
    chosen = mine[:, None, :] & (rank[:, None, :] == jnp.arange(capacity)[None, :, None])

    def chosen_of(values):
        return jnp.sum(jnp.where(chosen, values, 0), axis=2).reshape(-1)

    plan = jnp.concatenate(
        [
            sources,
            chosen_of(starts_all[:, None, :]),
            jnp.where(remaining_device, chosen_of(sizes_all[:, None, :]), 0),
            chosen_of(index[None, None, :] + 1) - 1,
        ]
    )
    plan_shape = (instances, capacity)

    local_output = attend(own_keys, own_values, cache_length, queries, own_fresh_k, own_fresh_v)
    near_sizes = list(range(step, most - cut, step)) + [most - cut]
    far_sizes = list(range(4 * step, most - cut, 4 * step)) + [most - cut]
    rests, pool = prepare(rest, near_sizes, (slot_count, 2, span_rows, group_width))
    local_output, pool, rests, extents, plan = lax.optimization_barrier(
        (local_output, pool, rests, extents, plan)
    )
    inherited = place(plan, *plan_shape, spread(local_output, all_steps, halved_count))
    first, inherited = lax.optimization_barrier((first, inherited))
    inherited = down(inherited)
    far_first = across(first, all_steps[0], 0)

    def finish(more, far, rests, first, plan, pool):
        if more:
            piece = down(rests[near_sizes.index(more)])
        near_first = [part for part, _ in spread(first, all_steps[1:])[1:]]
        if more:
            pieces = spread(piece, all_steps if far else all_steps[1:])
            pool = unpack(plan, *plan_shape, pieces, pool, cut, cut + more)
        return pool, near_first

    branches = [functools.partial(finish, more, False) for more in [0] + near_sizes]
    branches += [functools.partial(finish, more, True) for more in far_sizes]
    extra = jnp.maximum(extents[0] - cut, 0)
    near_choice = jnp.minimum((extra + step - 1) // step, len(near_sizes))
    far_choice = jnp.clip((extra + 4 * step - 1) // (4 * step) - 1, 0, len(far_sizes) - 1)
    choice = jnp.where(extents[1] > cut, 1 + len(near_sizes) + far_choice, near_choice)
    pool, near_first = lax.switch(choice, branches, rests, first, plan, pool)
    far_first, pool, inherited = lax.optimization_barrier((far_first, pool, inherited))
    places = [0]
    for stride in all_steps[1:]:
        places = places + [o ^ stride for o in places]
    near_parts = [(part, order.index(o)) for part, o in zip([first] + near_first, places)]
    far_parts = [
        (part, order.index(order[number] ^ all_steps[0]))
        for part, number in spread(far_first, all_steps[1:])
    ]
    kept_cache = unpack(plan, *plan_shape, near_parts + far_parts, pool, 0, cut)
    local_output = jnp.where(remaining_device, local_output, jnp.zeros_like(local_output))
    return (local_output, inherited[None, None], kept_cache[None, None])


def solution(mesh):
    placed = (
        P(("groups", "inst"), None, None),
        P(("groups", "inst"), None, "tp"),
        P(("groups", "inst"), None, "tp"),
        P(("groups", "inst"), None, "tp"),
        P(("groups", "inst"), None),
        P(("groups", "inst")),
        P(("groups", "inst"), None),
        P(None, "tp"),
        P(None, "tp"),
    )
    return jax.shard_map(
        local,
        mesh=mesh,
        in_specs=placed,
        out_specs=(
            P(("groups", "inst"), None, "tp"),
            P(("groups", "inst"), "tp", None, None, None),
            P(("groups", "inst"), "tp", None, None, None, None),
        ),
        check_vma=False,
    )
```

```python
import functools

import jax
import jax.numpy as jnp
from jax import lax
from jax.experimental import pallas as pl
from jax.experimental.pallas import tpu as pltpu
from jax.sharding import PartitionSpec as P

HD = 128
ROTARY_BASE = 500000.0
UNIT = 16
FIRST, STEP = 18, 2
ANY = pl.BlockSpec(memory_space=pl.ANY)
HBM = pl.BlockSpec(memory_space=pltpu.HBM)
VMEM_LIMIT = 60 * 1024 * 1024
UNPACK_LIMIT = 12 * 1024 * 1024


def rotate(values, positions):
    head_width = values.shape[-1]
    half_width = head_width // 2
    frequency = ROTARY_BASE ** (-(jnp.arange(half_width, dtype=jnp.float32) * 2.0 / head_width))
    angles = positions[..., None, None] * frequency
    cosine = jnp.cos(angles)
    sine_part = jnp.sin(angles)
    first_half = values[..., :half_width]
    second_half = values[..., half_width:]
    return jnp.concatenate(
        [
            first_half * cosine - second_half * sine_part,
            second_half * cosine + first_half * sine_part,
        ],
        axis=-1,
    )


def new_tokens(hidden, weight_key, weight_value, lengths):
    count = hidden.shape[0]
    flat_rows = hidden.reshape(count * 2, hidden.shape[-1])
    raw_keys = lax.optimization_barrier(
        jnp.dot(flat_rows, weight_key, preferred_element_type=jnp.float32)
    ).reshape(count, 2, -1, HD)
    positions = lengths.astype(jnp.float32)[:, None] + jnp.arange(2, dtype=jnp.float32)[None, :]
    fresh_keys = rotate(raw_keys, positions).reshape(count, 2, -1).astype(jnp.bfloat16)
    fresh_values = (
        jnp.dot(flat_rows, weight_value, preferred_element_type=jnp.float32)
        .reshape(count, 2, -1)
        .astype(jnp.bfloat16)
    )
    return (fresh_keys, fresh_values)


def attend(key_rows, value_rows, lengths, query_rows, fresh_keys, fresh_values):
    count = key_rows.shape[0]
    span_rows = key_rows.shape[1]
    head_groups = key_rows.shape[-1] // HD
    per_group = query_rows.shape[-1] // (head_groups * HD)
    query_heads = query_rows.reshape(count, 2, head_groups, per_group, HD)
    cache_keys = key_rows.reshape(count, span_rows, head_groups, HD)
    cache_values = value_rows.reshape(count, span_rows, head_groups, HD)
    new_keys = fresh_keys.reshape(count, 2, head_groups, HD)
    new_values = fresh_values.reshape(count, 2, head_groups, HD)
    scaling = HD ** (-0.5)
    cache_scores = (
        jnp.einsum("sjgqe,stge->sjgqt", query_heads, cache_keys, preferred_element_type=jnp.float32)
        * scaling
    )
    live_mask = jnp.arange(span_rows)[None, :] < lengths[:, None]
    cache_scores = jnp.where(live_mask[:, None, None, None, :], cache_scores, -jnp.inf)
    fresh_scores = (
        jnp.einsum("sjgqe,sige->sjgqi", query_heads, new_keys, preferred_element_type=jnp.float32)
        * scaling
    )
    allowed = jnp.arange(2)[None, :] <= jnp.arange(2)[:, None]
    fresh_scores = jnp.where(allowed[None, :, None, None, :], fresh_scores, -jnp.inf)
    highest = jnp.maximum(jnp.max(cache_scores, axis=-1), jnp.max(fresh_scores, axis=-1))
    cache_mass = jnp.exp(cache_scores - highest[..., None])
    fresh_mass = jnp.exp(fresh_scores - highest[..., None])
    total_mass = jnp.sum(cache_mass, axis=-1) + jnp.sum(fresh_mass, axis=-1)
    cache_weights = (cache_mass / total_mass[..., None]).astype(jnp.bfloat16)
    fresh_weights = (fresh_mass / total_mass[..., None]).astype(jnp.bfloat16)
    final_output = jnp.einsum(
        "sjgqt,stge->sjgqe", cache_weights, cache_values, preferred_element_type=jnp.float32
    )
    final_output = final_output + jnp.einsum(
        "sjgqi,sige->sjgqe", fresh_weights, new_values, preferred_element_type=jnp.float32
    )
    return final_output.reshape(count, 2, -1).astype(jnp.bfloat16)


def padded(lengths):
    return (lengths + (UNIT - 1)) // UNIT * UNIT


def strides(count):
    bits = []
    step = count // 2
    while step:
        bits.append(step)
        step //= 2
    return bits


def nearness(apart, steps):
    return sum((apart < step).astype(jnp.int32) for step in steps)


def pack_kernel(cuts, steps, table, lens, owners, keys, values, *refs):
    parts = refs[: len(cuts)]
    pools, pile, arrived, left_sems = refs[len(cuts) :]
    count, pages_most = lens.shape[0], table.shape[0]
    block = keys.shape[1]
    row = lax.broadcasted_iota(jnp.int32, (UNIT, keys.shape[2]), 0)
    me = lax.axis_index("inst")
    loads = [
        pltpu.make_async_copy(pool, pools.at[index], arrived.at[index])
        for index, pool in enumerate((keys, values))
    ]
    for load in loads:
        load.start()
    for load in loads:
        load.wait()

    def turn(i, start):
        r = lax.rem(i, count)
        live = lens[r]
        here = nearness(jnp.bitwise_xor(owners[r], me), steps) == i // count

        @pl.when(here)
        def _():
            for page in range(pages_most):

                @pl.when(live > page * block)
                def _():
                    source = table[page, r]
                    place = pl.ds(pl.multiple_of(start + page * block, UNIT), block)
                    for index in range(2):
                        pile[index, place, :] = pools[index, source]

            ending = padded(live) - UNIT
            place = pl.ds(pl.multiple_of(start + ending, UNIT), UNIT)
            mask = row < live - ending
            for index in range(2):
                kept = pile[index, place, :]
                pile[index, place, :] = jnp.where(mask, kept, jnp.zeros_like(kept))

        return start + jnp.where(here, padded(live), 0)

    lax.fori_loop(0, count * (len(steps) + 1), turn, jnp.int32(0))
    leaving = [
        pltpu.make_async_copy(
            pile.at[:, pl.ds(low, high - low), :], parts[number], left_sems.at[number]
        )
        for number, (low, high) in enumerate(cuts)
    ]
    for copy in leaving:
        copy.start()
    for copy in leaving:
        copy.wait()


def pack(page_table, lengths, owners, key_pool, value_pool, cuts, steps):
    width = key_pool.shape[2]
    block = key_pool.shape[1]
    return pl.pallas_call(
        functools.partial(pack_kernel, cuts, steps),
        out_shape=tuple(
            jax.ShapeDtypeStruct((2, high - low, width), jnp.bfloat16) for low, high in cuts
        ),
        grid_spec=pltpu.PrefetchScalarGridSpec(
            num_scalar_prefetch=3,
            grid=(),
            in_specs=[HBM, HBM],
            out_specs=[HBM] * len(cuts),
            scratch_shapes=[
                pltpu.VMEM((2,) + key_pool.shape, jnp.bfloat16),
                pltpu.VMEM((2, cuts[-1][1] + block, width), jnp.bfloat16),
                pltpu.SemaphoreType.DMA((2,)),
                pltpu.SemaphoreType.DMA((len(cuts),)),
            ],
        ),
        compiler_params=pltpu.CompilerParams(vmem_limit_bytes=VMEM_LIMIT),
        name="pack",
    )(page_table.T, lengths, owners, key_pool, value_pool)


def prepare_kernel(count, pile, *refs):
    parts, pool = refs[:count], refs[count]
    held, blank, arrived, sems, pool_sems = refs[count + 1 :]
    load = pltpu.make_async_copy(pile, held, arrived)
    load.start()
    blank[...] = jnp.zeros_like(blank)
    copies = [
        pltpu.make_async_copy(blank, pool.at[0, 0, slot], pool_sems.at[slot])
        for slot in range(pool.shape[2])
    ]
    for copy in copies:
        copy.start()
    load.wait()
    copies += [
        pltpu.make_async_copy(held.at[:, pl.ds(0, part.shape[1]), :], part, sems.at[number])
        for number, part in enumerate(parts)
    ]
    for copy in copies[pool.shape[2] :]:
        copy.start()
    for copy in copies:
        copy.wait()


def prepare(pile, sizes, pool_shape):
    *parts, pool = pl.pallas_call(
        functools.partial(prepare_kernel, len(sizes)),
        out_shape=[
            jax.ShapeDtypeStruct((2, size, pile.shape[2]), pile.dtype) for size in sizes
        ]
        + [jax.ShapeDtypeStruct(pool_shape, pile.dtype)],
        in_specs=[HBM],
        out_specs=[HBM] * (len(sizes) + 1),
        scratch_shapes=[
            pltpu.VMEM(pile.shape, pile.dtype),
            pltpu.VMEM(pool_shape[3:], pile.dtype),
            pltpu.SemaphoreType.DMA,
            pltpu.SemaphoreType.DMA((len(sizes),)),
            pltpu.SemaphoreType.DMA((pool_shape[2],)),
        ],
        compiler_params=pltpu.CompilerParams(vmem_limit_bytes=VMEM_LIMIT),
        name="prepare",
    )(pile)
    return parts, pool


def entry(plan, count, capacity, kind, j, c):
    return plan[count + (kind * count + j) * capacity + c]


def unpack_kernel(extents, total, capacity, numbers, plan, *refs):
    count = len(numbers)
    piles, out, stage, inward, outward = refs[:count], refs[-4], refs[-3], refs[-2], refs[-1]

    def span(k, c):
        j, (low, high) = numbers[k], extents[k]
        start = entry(plan, total, capacity, 0, j, c)
        begin = jnp.maximum(start, low)
        end = jnp.minimum(start + entry(plan, total, capacity, 1, j, c), high)
        return start, begin, end - begin

    def arriving(k, c):
        _, begin, rows = span(k, c)
        rows = pl.multiple_of(rows, UNIT)
        return pltpu.make_async_copy(
            piles[k].at[:, pl.ds(pl.multiple_of(begin - extents[k][0], UNIT), rows), :],
            stage.at[k * capacity + c, :, pl.ds(0, rows), :],
            inward.at[k * capacity + c],
        )

    def leaving(k, c):
        start, begin, rows = span(k, c)
        rows = pl.multiple_of(rows, UNIT)
        return pltpu.make_async_copy(
            stage.at[k * capacity + c, :, pl.ds(0, rows), :],
            out.at[
                0,
                0,
                plan[numbers[k]] * capacity + c,
                :,
                pl.ds(pl.multiple_of(begin - start, UNIT), rows),
                :,
            ],
            outward.at[k * capacity + c],
        )

    def each(action):
        for k in range(count):

            def slot(c, carry):
                @pl.when(span(k, c)[2] > 0)
                def _():
                    action(k, c)

                return carry

            lax.fori_loop(0, capacity, slot, 0)

    def turn(k, c):
        arriving(k, c).wait()
        leaving(k, c).start()

    each(lambda k, c: arriving(k, c).start())
    each(turn)
    each(lambda k, c: leaving(k, c).wait())


def unpack(plan, total, capacity, parts, out):
    count = len(parts)
    numbers = [part[1] for part in parts]
    extents = [part[2:] for part in parts]
    return pl.pallas_call(
        functools.partial(unpack_kernel, extents, total, capacity, numbers),
        out_shape=jax.ShapeDtypeStruct(out.shape, out.dtype),
        grid_spec=pltpu.PrefetchScalarGridSpec(
            num_scalar_prefetch=1,
            grid=(),
            in_specs=[ANY] * count + [HBM],
            out_specs=HBM,
            scratch_shapes=[
                pltpu.VMEM((count * capacity,) + out.shape[3:], out.dtype),
                pltpu.SemaphoreType.DMA((count * capacity,)),
                pltpu.SemaphoreType.DMA((count * capacity,)),
            ],
        ),
        input_output_aliases={1 + count: 0},
        compiler_params=pltpu.CompilerParams(vmem_limit_bytes=UNPACK_LIMIT),
        name="unpack",
    )(plan, *[part[0] for part in parts], out)


def place_kernel(total, capacity, numbers, plan, *refs):
    out = refs[-1]
    out[...] = jnp.zeros_like(out)
    for k, j in enumerate(numbers):

        def slot(c, carry):
            r = entry(plan, total, capacity, 2, j, c)

            @pl.when(r >= 0)
            def _():
                out[plan[j] * capacity + c] = refs[k][r]

            return carry

        lax.fori_loop(0, capacity, slot, 0)


def place(plan, total, capacity, parts):
    source = parts[0][0].shape
    shape = (total * capacity,) + source[1:]
    return pl.pallas_call(
        functools.partial(place_kernel, total, capacity, [number for _, number in parts]),
        out_shape=jax.ShapeDtypeStruct(shape, jnp.bfloat16),
        grid_spec=pltpu.PrefetchScalarGridSpec(
            num_scalar_prefetch=1,
            grid=(1,),
            in_specs=[pl.BlockSpec(source, lambda i, *_: (0, 0, 0))] * len(parts),
            out_specs=pl.BlockSpec(shape, lambda i, *_: (0, 0, 0)),
        ),
        compiler_params=pltpu.CompilerParams(vmem_limit_bytes=VMEM_LIMIT),
        name="place",
    )(plan, *[part for part, _ in parts])


def local(
    hidden_rows,
    queries,
    key_pool,
    value_pool,
    page_table,
    cache_length,
    new_owner,
    key_weight,
    value_weight,
):
    tp = lax.axis_size("tp")
    halved_count = tp // 2
    remaining_device = lax.axis_index("tp") < halved_count
    instances = lax.axis_size("inst")
    groups = lax.axis_size("groups")
    me = lax.axis_index("inst")
    requests = cache_length.shape[0]
    pages_most = page_table.shape[1]
    block_rows = key_pool.shape[1]
    group_width = key_pool.shape[2]
    capacity = max(2, 3 * requests // (2 * instances))
    slot_count = instances * capacity
    span_rows = pages_most * block_rows
    most = span_rows + (requests - 1) * (pages_most * 5 // 8) * block_rows
    step = STEP * block_rows
    cut = min(most, FIRST * block_rows)
    all_steps = strides(instances)
    order = [0]
    for stride in all_steps:
        order = order + [o ^ stride for o in order]

    def down(value):
        return lax.ppermute(value, "tp", [(t + halved_count, t) for t in range(halved_count)])

    def across(value, stride, low):
        pairs = [
            (i * tp + t, (i ^ stride) * tp + t)
            for i in range(instances)
            for t in range(low, low + halved_count)
        ]
        return lax.ppermute(value, ("inst", "tp"), pairs)

    def spread(value, steps, low=0):
        parts = [(value, 0)]
        for stride in steps:
            parts = parts + [(across(part, stride, low), o ^ stride) for part, o in parts]
        return [(part, order.index(o)) for part, o in parts]

    first, rest = pack(
        page_table,
        cache_length,
        new_owner[:, 0],
        key_pool,
        value_pool,
        [(0, cut), (cut, most)],
        all_steps,
    )
    sample = down(first[:1, :UNIT, :HD])
    first = down(first)
    _, rest, hidden_rows, lengths, new_owner, page_table = lax.optimization_barrier(
        (sample, rest, hidden_rows, cache_length, new_owner, page_table)
    )
    own_keys = key_pool[page_table].reshape(requests, span_rows, group_width)
    own_values = value_pool[page_table].reshape(requests, span_rows, group_width)
    own_fresh_k, own_fresh_v = new_tokens(hidden_rows, key_weight, value_weight, lengths)

    facts = jnp.stack([lengths, new_owner[:, 0]])[None]
    for stride in all_steps:
        facts = jnp.concatenate(
            [facts, lax.ppermute(facts, "inst", [(i, i ^ stride) for i in range(instances)])]
        )
    sources = me ^ jnp.array(order, jnp.int32)
    sizes_all = padded(facts[:, 0])
    near = nearness(facts[:, 1] ^ sources[:, None], all_steps)
    extents = jnp.stack(
        [
            jnp.max(jnp.sum(sizes_all, axis=1)),
            jnp.max(jnp.sum(jnp.where(near == 0, sizes_all, 0), axis=1)),
        ]
    )
    for stride in strides(groups):
        extents = jnp.maximum(
            extents,
            lax.ppermute(extents, "groups", [(g, g ^ stride) for g in range(groups)]),
        )
    mine = facts[:, 1] == me
    index = jnp.arange(requests)
    earlier = index[None, :] < index[:, None]
    packed_earlier = (near[:, None, :] < near[:, :, None]) | (
        (near[:, None, :] == near[:, :, None]) & earlier[None]
    )
    starts_all = jnp.sum(jnp.where(packed_earlier, sizes_all[:, None, :], 0), axis=2)
    rank = jnp.sum(jnp.where(earlier[None], mine[:, None, :].astype(jnp.int32), 0), axis=2)
    chosen = mine[:, None, :] & (rank[:, None, :] == jnp.arange(capacity)[None, :, None])

    def chosen_of(values):
        return jnp.sum(jnp.where(chosen, values, 0), axis=2).reshape(-1)

    plan = jnp.concatenate(
        [
            sources,
            chosen_of(starts_all[:, None, :]),
            jnp.where(remaining_device, chosen_of(sizes_all[:, None, :]), 0),
            chosen_of(index[None, None, :] + 1) - 1,
        ]
    )
    plan_shape = (instances, capacity)

    local_output = attend(own_keys, own_values, cache_length, queries, own_fresh_k, own_fresh_v)
    near_sizes = list(range(2 * step, (most - cut) * 3 // 4, step)) + [most - cut]
    far_sizes = near_sizes[2::2]
    rests, pool = prepare(rest, near_sizes, (1, 1, slot_count, 2, span_rows, group_width))
    local_output, pool, rests, extents, plan = lax.optimization_barrier(
        (local_output, pool, rests, extents, plan)
    )
    local_rows = local_output
    local_output = jnp.where(remaining_device, local_output, jnp.zeros_like(local_output))
    first, local_rows, local_output = lax.optimization_barrier((first, local_rows, local_output))

    def finish(more, far, rests, first, local_rows, plan, pool):
        piece = down(rests[near_sizes.index(more)])
        away = across(first, all_steps[0], 0)
        inherited = place(plan, *plan_shape, spread(local_rows, all_steps, halved_count))
        inherited = down(inherited)
        inherited = jnp.where(remaining_device, inherited, jnp.zeros_like(inherited))
        parts = [part + (0, cut) for part in spread(first, all_steps[1:])]
        pool = unpack(plan, *plan_shape, parts, pool)
        away, piece, pool, inherited = lax.optimization_barrier((away, piece, pool, inherited))
        parts = [
            (part, order.index(order[number] ^ all_steps[0]), 0, cut)
            for part, number in spread(away, all_steps[1:])
        ]
        pieces = [
            part + (cut, cut + more)
            for part in spread(piece, all_steps if far else all_steps[1:])
        ]
        pool = unpack(plan, *plan_shape, [parts[0], pieces[0]], pool)
        return inherited, unpack(plan, *plan_shape, parts[1:] + pieces[1:], pool)

    branches = [functools.partial(finish, more, False) for more in near_sizes]
    branches += [functools.partial(finish, more, True) for more in far_sizes]
    extra = jnp.maximum(extents[0] - cut, 0)
    near_choice = sum((extra > size).astype(jnp.int32) for size in near_sizes[:-1])
    far_choice = sum((extra > size).astype(jnp.int32) for size in far_sizes[:-1])
    choice = jnp.where(extents[1] > cut, len(near_sizes) + far_choice, near_choice)
    inherited, kept_cache = lax.switch(choice, branches, rests, first, local_rows, plan, pool)
    return (local_output, inherited[None, None], kept_cache)


def solution(mesh):
    placed = (
        P(("groups", "inst"), None, None),
        P(("groups", "inst"), None, "tp"),
        P(("groups", "inst"), None, "tp"),
        P(("groups", "inst"), None, "tp"),
        P(("groups", "inst"), None),
        P(("groups", "inst")),
        P(("groups", "inst"), None),
        P(None, "tp"),
        P(None, "tp"),
    )
    return jax.shard_map(
        local,
        mesh=mesh,
        in_specs=placed,
        out_specs=(
            P(("groups", "inst"), None, "tp"),
            P(("groups", "inst"), "tp", None, None, None),
            P(("groups", "inst"), "tp", None, None, None, None),
        ),
        check_vma=False,
    )
```

```python
import functools

import jax
import jax.numpy as jnp
from jax import lax
from jax.experimental import pallas as pl
from jax.experimental.pallas import tpu as pltpu
from jax.sharding import PartitionSpec as P

HD = 128
ROTARY_BASE = 500000.0
UNIT = 16
FIRST, STEP = 18, 2
ANY = pl.BlockSpec(memory_space=pl.ANY)
HBM = pl.BlockSpec(memory_space=pltpu.HBM)
VMEM_LIMIT = 60 * 1024 * 1024
UNPACK_LIMIT = 12 * 1024 * 1024


def rotate(values, positions):
    head_width = values.shape[-1]
    half_width = head_width // 2
    frequency = ROTARY_BASE ** (-(jnp.arange(half_width, dtype=jnp.float32) * 2.0 / head_width))
    angles = positions[..., None, None] * frequency
    cosine = jnp.cos(angles)
    sine_part = jnp.sin(angles)
    first_half = values[..., :half_width]
    second_half = values[..., half_width:]
    return jnp.concatenate(
        [
            first_half * cosine - second_half * sine_part,
            second_half * cosine + first_half * sine_part,
        ],
        axis=-1,
    )


def new_tokens(hidden, weight_key, weight_value, lengths):
    count = hidden.shape[0]
    flat_rows = hidden.reshape(count * 2, hidden.shape[-1])
    raw_keys = lax.optimization_barrier(
        jnp.dot(flat_rows, weight_key, preferred_element_type=jnp.float32)
    ).reshape(count, 2, -1, HD)
    positions = lengths.astype(jnp.float32)[:, None] + jnp.arange(2, dtype=jnp.float32)[None, :]
    fresh_keys = rotate(raw_keys, positions).reshape(count, 2, -1).astype(jnp.bfloat16)
    fresh_values = (
        jnp.dot(flat_rows, weight_value, preferred_element_type=jnp.float32)
        .reshape(count, 2, -1)
        .astype(jnp.bfloat16)
    )
    return (fresh_keys, fresh_values)


def attend(key_rows, value_rows, lengths, query_rows, fresh_keys, fresh_values):
    count = key_rows.shape[0]
    span_rows = key_rows.shape[1]
    head_groups = key_rows.shape[-1] // HD
    per_group = query_rows.shape[-1] // (head_groups * HD)
    query_heads = query_rows.reshape(count, 2, head_groups, per_group, HD)
    cache_keys = key_rows.reshape(count, span_rows, head_groups, HD)
    cache_values = value_rows.reshape(count, span_rows, head_groups, HD)
    new_keys = fresh_keys.reshape(count, 2, head_groups, HD)
    new_values = fresh_values.reshape(count, 2, head_groups, HD)
    scaling = HD ** (-0.5)
    cache_scores = (
        jnp.einsum("sjgqe,stge->sjgqt", query_heads, cache_keys, preferred_element_type=jnp.float32)
        * scaling
    )
    live_mask = jnp.arange(span_rows)[None, :] < lengths[:, None]
    cache_scores = jnp.where(live_mask[:, None, None, None, :], cache_scores, -jnp.inf)
    fresh_scores = (
        jnp.einsum("sjgqe,sige->sjgqi", query_heads, new_keys, preferred_element_type=jnp.float32)
        * scaling
    )
    allowed = jnp.arange(2)[None, :] <= jnp.arange(2)[:, None]
    fresh_scores = jnp.where(allowed[None, :, None, None, :], fresh_scores, -jnp.inf)
    highest = jnp.maximum(jnp.max(cache_scores, axis=-1), jnp.max(fresh_scores, axis=-1))
    cache_mass = jnp.exp(cache_scores - highest[..., None])
    fresh_mass = jnp.exp(fresh_scores - highest[..., None])
    total_mass = jnp.sum(cache_mass, axis=-1) + jnp.sum(fresh_mass, axis=-1)
    cache_weights = (cache_mass / total_mass[..., None]).astype(jnp.bfloat16)
    fresh_weights = (fresh_mass / total_mass[..., None]).astype(jnp.bfloat16)
    final_output = jnp.einsum(
        "sjgqt,stge->sjgqe", cache_weights, cache_values, preferred_element_type=jnp.float32
    )
    final_output = final_output + jnp.einsum(
        "sjgqi,sige->sjgqe", fresh_weights, new_values, preferred_element_type=jnp.float32
    )
    return final_output.reshape(count, 2, -1).astype(jnp.bfloat16)


def padded(lengths):
    return (lengths + (UNIT - 1)) // UNIT * UNIT


def strides(count):
    bits = []
    step = count // 2
    while step:
        bits.append(step)
        step //= 2
    return bits


def nearness(apart, steps):
    return sum((apart < step).astype(jnp.int32) for step in steps)


def pack_kernel(cuts, steps, table, lens, owners, keys, values, *refs):
    parts = refs[: len(cuts)]
    pools, pile, arrived, left_sems = refs[len(cuts) :]
    count, pages_most = lens.shape[0], table.shape[0]
    block = keys.shape[1]
    row = lax.broadcasted_iota(jnp.int32, (UNIT, keys.shape[2]), 0)
    me = lax.axis_index("inst")
    loads = [
        pltpu.make_async_copy(pool, pools.at[index], arrived.at[index])
        for index, pool in enumerate((keys, values))
    ]
    for load in loads:
        load.start()
    for load in loads:
        load.wait()

    def turn(i, start):
        r = lax.rem(i, count)
        live = lens[r]
        here = nearness(jnp.bitwise_xor(owners[r], me), steps) == i // count

        @pl.when(here)
        def _():
            for page in range(pages_most):

                @pl.when(live > page * block)
                def _():
                    source = table[page, r]
                    place = pl.ds(pl.multiple_of(start + page * block, UNIT), block)
                    for index in range(2):
                        pile[index, place, :] = pools[index, source]

            ending = padded(live) - UNIT
            place = pl.ds(pl.multiple_of(start + ending, UNIT), UNIT)
            mask = row < live - ending
            for index in range(2):
                kept = pile[index, place, :]
                pile[index, place, :] = jnp.where(mask, kept, jnp.zeros_like(kept))

        return start + jnp.where(here, padded(live), 0)

    lax.fori_loop(0, count * (len(steps) + 1), turn, jnp.int32(0))
    leaving = [
        pltpu.make_async_copy(
            pile.at[:, pl.ds(low, high - low), :], parts[number], left_sems.at[number]
        )
        for number, (low, high) in enumerate(cuts)
    ]
    for copy in leaving:
        copy.start()
    for copy in leaving:
        copy.wait()


def pack(page_table, lengths, owners, key_pool, value_pool, cuts, steps):
    width = key_pool.shape[2]
    block = key_pool.shape[1]
    return pl.pallas_call(
        functools.partial(pack_kernel, cuts, steps),
        out_shape=tuple(
            jax.ShapeDtypeStruct((2, high - low, width), jnp.bfloat16) for low, high in cuts
        ),
        grid_spec=pltpu.PrefetchScalarGridSpec(
            num_scalar_prefetch=3,
            grid=(),
            in_specs=[HBM, HBM],
            out_specs=[HBM] * len(cuts),
            scratch_shapes=[
                pltpu.VMEM((2,) + key_pool.shape, jnp.bfloat16),
                pltpu.VMEM((2, cuts[-1][1] + block, width), jnp.bfloat16),
                pltpu.SemaphoreType.DMA((2,)),
                pltpu.SemaphoreType.DMA((len(cuts),)),
            ],
        ),
        compiler_params=pltpu.CompilerParams(vmem_limit_bytes=VMEM_LIMIT),
        name="pack",
    )(page_table.T, lengths, owners, key_pool, value_pool)


def prepare_kernel(count, pile, *refs):
    parts, pool = refs[:count], refs[count]
    held, blank, arrived, sems, pool_sems = refs[count + 1 :]
    load = pltpu.make_async_copy(pile, held, arrived)
    load.start()
    blank[...] = jnp.zeros_like(blank)
    copies = [
        pltpu.make_async_copy(blank, pool.at[0, 0, slot], pool_sems.at[slot])
        for slot in range(pool.shape[2])
    ]
    for copy in copies:
        copy.start()
    load.wait()
    copies += [
        pltpu.make_async_copy(held.at[:, pl.ds(0, part.shape[1]), :], part, sems.at[number])
        for number, part in enumerate(parts)
    ]
    for copy in copies[pool.shape[2] :]:
        copy.start()
    for copy in copies:
        copy.wait()


def prepare(pile, sizes, pool_shape):
    *parts, pool = pl.pallas_call(
        functools.partial(prepare_kernel, len(sizes)),
        out_shape=[
            jax.ShapeDtypeStruct((2, size, pile.shape[2]), pile.dtype) for size in sizes
        ]
        + [jax.ShapeDtypeStruct(pool_shape, pile.dtype)],
        in_specs=[HBM],
        out_specs=[HBM] * (len(sizes) + 1),
        scratch_shapes=[
            pltpu.VMEM(pile.shape, pile.dtype),
            pltpu.VMEM(pool_shape[3:], pile.dtype),
            pltpu.SemaphoreType.DMA,
            pltpu.SemaphoreType.DMA((len(sizes),)),
            pltpu.SemaphoreType.DMA((pool_shape[2],)),
        ],
        compiler_params=pltpu.CompilerParams(vmem_limit_bytes=VMEM_LIMIT),
        name="prepare",
    )(pile)
    return parts, pool


def entry(plan, count, capacity, kind, j, c):
    return plan[count + (kind * count + j) * capacity + c]


def unpack_kernel(extents, total, capacity, numbers, plan, *refs):
    count = len(numbers)
    piles, out, stage, inward, outward = refs[:count], refs[-4], refs[-3], refs[-2], refs[-1]

    def span(k, c):
        j, (low, high) = numbers[k], extents[k]
        start = entry(plan, total, capacity, 0, j, c)
        begin = jnp.maximum(start, low)
        end = jnp.minimum(start + entry(plan, total, capacity, 1, j, c), high)
        return start, begin, end - begin

    def arriving(k, c):
        _, begin, rows = span(k, c)
        rows = pl.multiple_of(rows, UNIT)
        return pltpu.make_async_copy(
            piles[k].at[:, pl.ds(pl.multiple_of(begin - extents[k][0], UNIT), rows), :],
            stage.at[k * capacity + c, :, pl.ds(0, rows), :],
            inward.at[k * capacity + c],
        )

    def leaving(k, c):
        start, begin, rows = span(k, c)
        rows = pl.multiple_of(rows, UNIT)
        return pltpu.make_async_copy(
            stage.at[k * capacity + c, :, pl.ds(0, rows), :],
            out.at[
                0,
                0,
                plan[numbers[k]] * capacity + c,
                :,
                pl.ds(pl.multiple_of(begin - start, UNIT), rows),
                :,
            ],
            outward.at[k * capacity + c],
        )

    def each(action):
        for k in range(count):

            def slot(c, carry):
                @pl.when(span(k, c)[2] > 0)
                def _():
                    action(k, c)

                return carry

            lax.fori_loop(0, capacity, slot, 0)

    def turn(k, c):
        arriving(k, c).wait()
        leaving(k, c).start()

    each(lambda k, c: arriving(k, c).start())
    each(turn)
    each(lambda k, c: leaving(k, c).wait())


def unpack(plan, total, capacity, parts, out):
    count = len(parts)
    numbers = [part[1] for part in parts]
    extents = [part[2:] for part in parts]
    return pl.pallas_call(
        functools.partial(unpack_kernel, extents, total, capacity, numbers),
        out_shape=jax.ShapeDtypeStruct(out.shape, out.dtype),
        grid_spec=pltpu.PrefetchScalarGridSpec(
            num_scalar_prefetch=1,
            grid=(),
            in_specs=[ANY] * count + [HBM],
            out_specs=HBM,
            scratch_shapes=[
                pltpu.VMEM((count * capacity,) + out.shape[3:], out.dtype),
                pltpu.SemaphoreType.DMA((count * capacity,)),
                pltpu.SemaphoreType.DMA((count * capacity,)),
            ],
        ),
        input_output_aliases={1 + count: 0},
        compiler_params=pltpu.CompilerParams(vmem_limit_bytes=UNPACK_LIMIT),
        name="unpack",
    )(plan, *[part[0] for part in parts], out)


def place_kernel(total, capacity, numbers, plan, *refs):
    out = refs[-1]
    out[...] = jnp.zeros_like(out)
    for k, j in enumerate(numbers):

        def slot(c, carry):
            r = entry(plan, total, capacity, 2, j, c)

            @pl.when(r >= 0)
            def _():
                out[plan[j] * capacity + c] = refs[k][r]

            return carry

        lax.fori_loop(0, capacity, slot, 0)


def place(plan, total, capacity, parts):
    source = parts[0][0].shape
    shape = (total * capacity,) + source[1:]
    return pl.pallas_call(
        functools.partial(place_kernel, total, capacity, [number for _, number in parts]),
        out_shape=jax.ShapeDtypeStruct(shape, jnp.bfloat16),
        grid_spec=pltpu.PrefetchScalarGridSpec(
            num_scalar_prefetch=1,
            grid=(1,),
            in_specs=[pl.BlockSpec(source, lambda i, *_: (0, 0, 0))] * len(parts),
            out_specs=pl.BlockSpec(shape, lambda i, *_: (0, 0, 0)),
        ),
        compiler_params=pltpu.CompilerParams(vmem_limit_bytes=VMEM_LIMIT),
        name="place",
    )(plan, *[part for part, _ in parts])


def local(
    hidden_rows,
    queries,
    key_pool,
    value_pool,
    page_table,
    cache_length,
    new_owner,
    key_weight,
    value_weight,
):
    tp = lax.axis_size("tp")
    halved_count = tp // 2
    remaining_device = lax.axis_index("tp") < halved_count
    instances = lax.axis_size("inst")
    groups = lax.axis_size("groups")
    me = lax.axis_index("inst")
    requests = cache_length.shape[0]
    pages_most = page_table.shape[1]
    block_rows = key_pool.shape[1]
    group_width = key_pool.shape[2]
    capacity = max(2, 3 * requests // (2 * instances))
    slot_count = instances * capacity
    span_rows = pages_most * block_rows
    most = span_rows + (requests - 1) * (pages_most * 5 // 8) * block_rows
    step = STEP * block_rows
    cut = min(most, FIRST * block_rows)
    all_steps = strides(instances)
    order = [0]
    for stride in all_steps:
        order = order + [o ^ stride for o in order]

    def down(value):
        return lax.ppermute(value, "tp", [(t + halved_count, t) for t in range(halved_count)])

    def across(value, stride, low):
        pairs = [
            (i * tp + t, (i ^ stride) * tp + t)
            for i in range(instances)
            for t in range(low, low + halved_count)
        ]
        return lax.ppermute(value, ("inst", "tp"), pairs)

    def spread(value, steps, low=0):
        parts = [(value, 0)]
        for stride in steps:
            parts = parts + [(across(part, stride, low), o ^ stride) for part, o in parts]
        return [(part, order.index(o)) for part, o in parts]

    first, rest = pack(
        page_table,
        cache_length,
        new_owner[:, 0],
        key_pool,
        value_pool,
        [(0, cut), (cut, most)],
        all_steps,
    )
    sample = down(first[:1, :UNIT, :HD])
    first = down(first)
    _, rest, hidden_rows, lengths, new_owner, page_table = lax.optimization_barrier(
        (sample, rest, hidden_rows, cache_length, new_owner, page_table)
    )
    own_keys = key_pool[page_table].reshape(requests, span_rows, group_width)
    own_values = value_pool[page_table].reshape(requests, span_rows, group_width)
    own_fresh_k, own_fresh_v = new_tokens(hidden_rows, key_weight, value_weight, lengths)

    facts = jnp.stack([lengths, new_owner[:, 0]])[None]
    for stride in all_steps:
        facts = jnp.concatenate(
            [facts, lax.ppermute(facts, "inst", [(i, i ^ stride) for i in range(instances)])]
        )
    sources = me ^ jnp.array(order, jnp.int32)
    sizes_all = padded(facts[:, 0])
    near = nearness(facts[:, 1] ^ sources[:, None], all_steps)
    extents = jnp.stack(
        [
            jnp.max(jnp.sum(sizes_all, axis=1)),
            jnp.max(jnp.sum(jnp.where(near == 0, sizes_all, 0), axis=1)),
        ]
    )
    for stride in strides(groups):
        extents = jnp.maximum(
            extents,
            lax.ppermute(extents, "groups", [(g, g ^ stride) for g in range(groups)]),
        )
    mine = facts[:, 1] == me
    index = jnp.arange(requests)
    earlier = index[None, :] < index[:, None]
    packed_earlier = (near[:, None, :] < near[:, :, None]) | (
        (near[:, None, :] == near[:, :, None]) & earlier[None]
    )
    starts_all = jnp.sum(jnp.where(packed_earlier, sizes_all[:, None, :], 0), axis=2)
    rank = jnp.sum(jnp.where(earlier[None], mine[:, None, :].astype(jnp.int32), 0), axis=2)
    chosen = mine[:, None, :] & (rank[:, None, :] == jnp.arange(capacity)[None, :, None])

    def chosen_of(values):
        return jnp.sum(jnp.where(chosen, values, 0), axis=2).reshape(-1)

    plan = jnp.concatenate(
        [
            sources,
            chosen_of(starts_all[:, None, :]),
            jnp.where(remaining_device, chosen_of(sizes_all[:, None, :]), 0),
            chosen_of(index[None, None, :] + 1) - 1,
        ]
    )
    plan_shape = (instances, capacity)

    local_output = attend(own_keys, own_values, cache_length, queries, own_fresh_k, own_fresh_v)
    near_sizes = list(range(3 * step, (most - cut) * 3 // 4, step)) + [most - cut]
    far_sizes = near_sizes[1:]
    rests, pool = prepare(rest, near_sizes, (1, 1, slot_count, 2, span_rows, group_width))
    local_output, pool, rests, extents, plan = lax.optimization_barrier(
        (local_output, pool, rests, extents, plan)
    )
    local_rows = local_output
    local_output = jnp.where(remaining_device, local_output, jnp.zeros_like(local_output))
    first, local_rows, local_output = lax.optimization_barrier((first, local_rows, local_output))

    def finish(more, far, rests, first, local_rows, plan, pool):
        piece = down(rests[near_sizes.index(more)])
        away = across(first, all_steps[0], 0)
        inherited = place(plan, *plan_shape, spread(local_rows, all_steps, halved_count))
        inherited = down(inherited)
        inherited = jnp.where(remaining_device, inherited, jnp.zeros_like(inherited))
        parts = [part + (0, cut) for part in spread(first, all_steps[1:])]
        pool = unpack(plan, *plan_shape, parts, pool)
        away, piece, pool, inherited = lax.optimization_barrier((away, piece, pool, inherited))
        parts = [
            (part, order.index(order[number] ^ all_steps[0]), 0, cut)
            for part, number in spread(away, all_steps[1:])
        ]
        pieces = [
            part + (cut, cut + more)
            for part in spread(piece, all_steps if far else all_steps[1:])
        ]
        pool = unpack(plan, *plan_shape, [parts[0], pieces[0]], pool)
        return inherited, unpack(plan, *plan_shape, parts[1:] + pieces[1:], pool)

    branches = [functools.partial(finish, more, False) for more in near_sizes]
    branches += [functools.partial(finish, more, True) for more in far_sizes]
    extra = jnp.maximum(extents[0] - cut, 0)
    near_choice = sum((extra > size).astype(jnp.int32) for size in near_sizes[:-1])
    far_choice = sum((extra > size).astype(jnp.int32) for size in far_sizes[:-1])
    choice = jnp.where(extents[1] > cut, len(near_sizes) + far_choice, near_choice)
    inherited, kept_cache = lax.switch(choice, branches, rests, first, local_rows, plan, pool)
    return (local_output, inherited[None, None], kept_cache)


def solution(mesh):
    placed = (
        P(("groups", "inst"), None, None),
        P(("groups", "inst"), None, "tp"),
        P(("groups", "inst"), None, "tp"),
        P(("groups", "inst"), None, "tp"),
        P(("groups", "inst"), None),
        P(("groups", "inst")),
        P(("groups", "inst"), None),
        P(None, "tp"),
        P(None, "tp"),
    )
    return jax.shard_map(
        local,
        mesh=mesh,
        in_specs=placed,
        out_specs=(
            P(("groups", "inst"), None, "tp"),
            P(("groups", "inst"), "tp", None, None, None),
            P(("groups", "inst"), "tp", None, None, None, None),
        ),
        check_vma=False,
    )
```

```python
import functools

import jax
import jax.numpy as jnp
from jax import lax
from jax.experimental import pallas as pl
from jax.experimental.pallas import tpu as pltpu
from jax.sharding import PartitionSpec as P

HD = 128
ROTARY_BASE = 500000.0
UNIT = 16
FIRST, STEP = 18, 1
ANY = pl.BlockSpec(memory_space=pl.ANY)
HBM = pl.BlockSpec(memory_space=pltpu.HBM)
VMEM_LIMIT = 60 * 1024 * 1024
UNPACK_LIMIT = 12 * 1024 * 1024


def rotate(values, positions):
    head_width = values.shape[-1]
    half_width = head_width // 2
    frequency = ROTARY_BASE ** (-(jnp.arange(half_width, dtype=jnp.float32) * 2.0 / head_width))
    angles = positions[..., None, None] * frequency
    cosine = jnp.cos(angles)
    sine_part = jnp.sin(angles)
    first_half = values[..., :half_width]
    second_half = values[..., half_width:]
    return jnp.concatenate(
        [
            first_half * cosine - second_half * sine_part,
            second_half * cosine + first_half * sine_part,
        ],
        axis=-1,
    )


def new_tokens(hidden, weight_key, weight_value, lengths):
    count = hidden.shape[0]
    flat_rows = hidden.reshape(count * 2, hidden.shape[-1])
    raw_keys = lax.optimization_barrier(
        jnp.dot(flat_rows, weight_key, preferred_element_type=jnp.float32)
    ).reshape(count, 2, -1, HD)
    positions = lengths.astype(jnp.float32)[:, None] + jnp.arange(2, dtype=jnp.float32)[None, :]
    fresh_keys = rotate(raw_keys, positions).reshape(count, 2, -1).astype(jnp.bfloat16)
    fresh_values = (
        jnp.dot(flat_rows, weight_value, preferred_element_type=jnp.float32)
        .reshape(count, 2, -1)
        .astype(jnp.bfloat16)
    )
    return (fresh_keys, fresh_values)


def attend(key_rows, value_rows, lengths, query_rows, fresh_keys, fresh_values):
    count = key_rows.shape[0]
    span_rows = key_rows.shape[1]
    head_groups = key_rows.shape[-1] // HD
    per_group = query_rows.shape[-1] // (head_groups * HD)
    query_heads = query_rows.reshape(count, 2, head_groups, per_group, HD)
    cache_keys = key_rows.reshape(count, span_rows, head_groups, HD)
    cache_values = value_rows.reshape(count, span_rows, head_groups, HD)
    new_keys = fresh_keys.reshape(count, 2, head_groups, HD)
    new_values = fresh_values.reshape(count, 2, head_groups, HD)
    scaling = HD ** (-0.5)
    cache_scores = (
        jnp.einsum("sjgqe,stge->sjgqt", query_heads, cache_keys, preferred_element_type=jnp.float32)
        * scaling
    )
    live_mask = jnp.arange(span_rows)[None, :] < lengths[:, None]
    cache_scores = jnp.where(live_mask[:, None, None, None, :], cache_scores, -jnp.inf)
    fresh_scores = (
        jnp.einsum("sjgqe,sige->sjgqi", query_heads, new_keys, preferred_element_type=jnp.float32)
        * scaling
    )
    allowed = jnp.arange(2)[None, :] <= jnp.arange(2)[:, None]
    fresh_scores = jnp.where(allowed[None, :, None, None, :], fresh_scores, -jnp.inf)
    highest = jnp.maximum(jnp.max(cache_scores, axis=-1), jnp.max(fresh_scores, axis=-1))
    cache_mass = jnp.exp(cache_scores - highest[..., None])
    fresh_mass = jnp.exp(fresh_scores - highest[..., None])
    total_mass = jnp.sum(cache_mass, axis=-1) + jnp.sum(fresh_mass, axis=-1)
    cache_weights = (cache_mass / total_mass[..., None]).astype(jnp.bfloat16)
    fresh_weights = (fresh_mass / total_mass[..., None]).astype(jnp.bfloat16)
    final_output = jnp.einsum(
        "sjgqt,stge->sjgqe", cache_weights, cache_values, preferred_element_type=jnp.float32
    )
    final_output = final_output + jnp.einsum(
        "sjgqi,sige->sjgqe", fresh_weights, new_values, preferred_element_type=jnp.float32
    )
    return final_output.reshape(count, 2, -1).astype(jnp.bfloat16)


def padded(lengths):
    return (lengths + (UNIT - 1)) // UNIT * UNIT


def strides(count):
    bits = []
    step = count // 2
    while step:
        bits.append(step)
        step //= 2
    return bits


def nearness(apart, steps):
    return sum((apart < step).astype(jnp.int32) for step in steps)


def pack_kernel(cuts, steps, table, lens, owners, keys, values, *refs):
    parts = refs[: len(cuts)]
    pools, pile, arrived, left_sems = refs[len(cuts) :]
    count, pages_most = lens.shape[0], table.shape[0]
    block = keys.shape[1]
    row = lax.broadcasted_iota(jnp.int32, (UNIT, keys.shape[2]), 0)
    me = lax.axis_index("inst")
    loads = [
        pltpu.make_async_copy(pool, pools.at[index], arrived.at[index])
        for index, pool in enumerate((keys, values))
    ]
    for load in loads:
        load.start()
    for load in loads:
        load.wait()

    def turn(i, start):
        r = lax.rem(i, count)
        live = lens[r]
        here = nearness(jnp.bitwise_xor(owners[r], me), steps) == i // count

        @pl.when(here)
        def _():
            for page in range(pages_most):

                @pl.when(live > page * block)
                def _():
                    source = table[page, r]
                    place = pl.ds(pl.multiple_of(start + page * block, UNIT), block)
                    for index in range(2):
                        pile[index, place, :] = pools[index, source]

            ending = padded(live) - UNIT
            place = pl.ds(pl.multiple_of(start + ending, UNIT), UNIT)
            mask = row < live - ending
            for index in range(2):
                kept = pile[index, place, :]
                pile[index, place, :] = jnp.where(mask, kept, jnp.zeros_like(kept))

        return start + jnp.where(here, padded(live), 0)

    lax.fori_loop(0, count * (len(steps) + 1), turn, jnp.int32(0))
    leaving = [
        pltpu.make_async_copy(
            pile.at[:, pl.ds(low, high - low), :], parts[number], left_sems.at[number]
        )
        for number, (low, high) in enumerate(cuts)
    ]
    for copy in leaving:
        copy.start()
    for copy in leaving:
        copy.wait()


def pack(page_table, lengths, owners, key_pool, value_pool, cuts, steps):
    width = key_pool.shape[2]
    block = key_pool.shape[1]
    return pl.pallas_call(
        functools.partial(pack_kernel, cuts, steps),
        out_shape=tuple(
            jax.ShapeDtypeStruct((2, high - low, width), jnp.bfloat16) for low, high in cuts
        ),
        grid_spec=pltpu.PrefetchScalarGridSpec(
            num_scalar_prefetch=3,
            grid=(),
            in_specs=[HBM, HBM],
            out_specs=[HBM] * len(cuts),
            scratch_shapes=[
                pltpu.VMEM((2,) + key_pool.shape, jnp.bfloat16),
                pltpu.VMEM((2, cuts[-1][1] + block, width), jnp.bfloat16),
                pltpu.SemaphoreType.DMA((2,)),
                pltpu.SemaphoreType.DMA((len(cuts),)),
            ],
        ),
        compiler_params=pltpu.CompilerParams(vmem_limit_bytes=VMEM_LIMIT),
        name="pack",
    )(page_table.T, lengths, owners, key_pool, value_pool)


def prepare_kernel(count, pile, *refs):
    parts, pool = refs[:count], refs[count]
    held, blank, arrived, sems, pool_sems = refs[count + 1 :]
    load = pltpu.make_async_copy(pile, held, arrived)
    load.start()
    blank[...] = jnp.zeros_like(blank)
    copies = [
        pltpu.make_async_copy(blank, pool.at[0, 0, slot], pool_sems.at[slot])
        for slot in range(pool.shape[2])
    ]
    for copy in copies:
        copy.start()
    load.wait()
    copies += [
        pltpu.make_async_copy(held.at[:, pl.ds(0, part.shape[1]), :], part, sems.at[number])
        for number, part in enumerate(parts)
    ]
    for copy in copies[pool.shape[2] :]:
        copy.start()
    for copy in copies:
        copy.wait()


def prepare(pile, sizes, pool_shape):
    *parts, pool = pl.pallas_call(
        functools.partial(prepare_kernel, len(sizes)),
        out_shape=[
            jax.ShapeDtypeStruct((2, size, pile.shape[2]), pile.dtype) for size in sizes
        ]
        + [jax.ShapeDtypeStruct(pool_shape, pile.dtype)],
        in_specs=[HBM],
        out_specs=[HBM] * (len(sizes) + 1),
        scratch_shapes=[
            pltpu.VMEM(pile.shape, pile.dtype),
            pltpu.VMEM(pool_shape[3:], pile.dtype),
            pltpu.SemaphoreType.DMA,
            pltpu.SemaphoreType.DMA((len(sizes),)),
            pltpu.SemaphoreType.DMA((pool_shape[2],)),
        ],
        compiler_params=pltpu.CompilerParams(vmem_limit_bytes=VMEM_LIMIT),
        name="prepare",
    )(pile)
    return parts, pool


def entry(plan, count, capacity, kind, j, c):
    return plan[count + (kind * count + j) * capacity + c]


def unpack_kernel(extents, total, capacity, numbers, plan, *refs):
    count = len(numbers)
    piles, out, stage, inward, outward = refs[:count], refs[-4], refs[-3], refs[-2], refs[-1]

    def span(k, c):
        j, (low, high) = numbers[k], extents[k]
        start = entry(plan, total, capacity, 0, j, c)
        begin = jnp.maximum(start, low)
        end = jnp.minimum(start + entry(plan, total, capacity, 1, j, c), high)
        return start, begin, end - begin

    def arriving(k, c):
        _, begin, rows = span(k, c)
        rows = pl.multiple_of(rows, UNIT)
        return pltpu.make_async_copy(
            piles[k].at[:, pl.ds(pl.multiple_of(begin - extents[k][0], UNIT), rows), :],
            stage.at[k * capacity + c, :, pl.ds(0, rows), :],
            inward.at[k * capacity + c],
        )

    def leaving(k, c):
        start, begin, rows = span(k, c)
        rows = pl.multiple_of(rows, UNIT)
        return pltpu.make_async_copy(
            stage.at[k * capacity + c, :, pl.ds(0, rows), :],
            out.at[
                0,
                0,
                plan[numbers[k]] * capacity + c,
                :,
                pl.ds(pl.multiple_of(begin - start, UNIT), rows),
                :,
            ],
            outward.at[k * capacity + c],
        )

    def each(action):
        for k in range(count):

            def slot(c, carry):
                @pl.when(span(k, c)[2] > 0)
                def _():
                    action(k, c)

                return carry

            lax.fori_loop(0, capacity, slot, 0)

    def turn(k, c):
        arriving(k, c).wait()
        leaving(k, c).start()

    each(lambda k, c: arriving(k, c).start())
    each(turn)
    each(lambda k, c: leaving(k, c).wait())


def unpack(plan, total, capacity, parts, out):
    count = len(parts)
    numbers = [part[1] for part in parts]
    extents = [part[2:] for part in parts]
    return pl.pallas_call(
        functools.partial(unpack_kernel, extents, total, capacity, numbers),
        out_shape=jax.ShapeDtypeStruct(out.shape, out.dtype),
        grid_spec=pltpu.PrefetchScalarGridSpec(
            num_scalar_prefetch=1,
            grid=(),
            in_specs=[ANY] * count + [HBM],
            out_specs=HBM,
            scratch_shapes=[
                pltpu.VMEM((count * capacity,) + out.shape[3:], out.dtype),
                pltpu.SemaphoreType.DMA((count * capacity,)),
                pltpu.SemaphoreType.DMA((count * capacity,)),
            ],
        ),
        input_output_aliases={1 + count: 0},
        compiler_params=pltpu.CompilerParams(vmem_limit_bytes=UNPACK_LIMIT),
        name="unpack",
    )(plan, *[part[0] for part in parts], out)


def place_kernel(total, capacity, numbers, plan, *refs):
    out = refs[-1]
    out[...] = jnp.zeros_like(out)
    for k, j in enumerate(numbers):

        def slot(c, carry):
            r = entry(plan, total, capacity, 2, j, c)

            @pl.when(r >= 0)
            def _():
                out[plan[j] * capacity + c] = refs[k][r]

            return carry

        lax.fori_loop(0, capacity, slot, 0)


def place(plan, total, capacity, parts):
    source = parts[0][0].shape
    shape = (total * capacity,) + source[1:]
    return pl.pallas_call(
        functools.partial(place_kernel, total, capacity, [number for _, number in parts]),
        out_shape=jax.ShapeDtypeStruct(shape, jnp.bfloat16),
        grid_spec=pltpu.PrefetchScalarGridSpec(
            num_scalar_prefetch=1,
            grid=(1,),
            in_specs=[pl.BlockSpec(source, lambda i, *_: (0, 0, 0))] * len(parts),
            out_specs=pl.BlockSpec(shape, lambda i, *_: (0, 0, 0)),
        ),
        compiler_params=pltpu.CompilerParams(vmem_limit_bytes=VMEM_LIMIT),
        name="place",
    )(plan, *[part for part, _ in parts])


def local(
    hidden_rows,
    queries,
    key_pool,
    value_pool,
    page_table,
    cache_length,
    new_owner,
    key_weight,
    value_weight,
):
    tp = lax.axis_size("tp")
    halved_count = tp // 2
    remaining_device = lax.axis_index("tp") < halved_count
    instances = lax.axis_size("inst")
    groups = lax.axis_size("groups")
    me = lax.axis_index("inst")
    requests = cache_length.shape[0]
    pages_most = page_table.shape[1]
    block_rows = key_pool.shape[1]
    group_width = key_pool.shape[2]
    capacity = max(2, 3 * requests // (2 * instances))
    slot_count = instances * capacity
    span_rows = pages_most * block_rows
    most = span_rows + (requests - 1) * (pages_most * 5 // 8) * block_rows
    step = STEP * block_rows
    cut = min(most, FIRST * block_rows)
    all_steps = strides(instances)
    order = [0]
    for stride in all_steps:
        order = order + [o ^ stride for o in order]

    def down(value):
        return lax.ppermute(value, "tp", [(t + halved_count, t) for t in range(halved_count)])

    def across(value, stride, low):
        pairs = [
            (i * tp + t, (i ^ stride) * tp + t)
            for i in range(instances)
            for t in range(low, low + halved_count)
        ]
        return lax.ppermute(value, ("inst", "tp"), pairs)

    def spread(value, steps, low=0):
        parts = [(value, 0)]
        for stride in steps:
            parts = parts + [(across(part, stride, low), o ^ stride) for part, o in parts]
        return [(part, order.index(o)) for part, o in parts]

    first, rest = pack(
        page_table,
        cache_length,
        new_owner[:, 0],
        key_pool,
        value_pool,
        [(0, cut), (cut, most)],
        all_steps,
    )
    sample = down(first[:1, :UNIT, :HD])
    first = down(first)
    _, rest, hidden_rows, lengths, new_owner, page_table = lax.optimization_barrier(
        (sample, rest, hidden_rows, cache_length, new_owner, page_table)
    )
    own_keys = key_pool[page_table].reshape(requests, span_rows, group_width)
    own_values = value_pool[page_table].reshape(requests, span_rows, group_width)
    own_fresh_k, own_fresh_v = new_tokens(hidden_rows, key_weight, value_weight, lengths)

    facts = jnp.stack([lengths, new_owner[:, 0]])[None]
    for stride in all_steps:
        facts = jnp.concatenate(
            [facts, lax.ppermute(facts, "inst", [(i, i ^ stride) for i in range(instances)])]
        )
    sources = me ^ jnp.array(order, jnp.int32)
    sizes_all = padded(facts[:, 0])
    near = nearness(facts[:, 1] ^ sources[:, None], all_steps)
    extents = jnp.stack(
        [
            jnp.max(jnp.sum(sizes_all, axis=1)),
            jnp.max(jnp.sum(jnp.where(near == 0, sizes_all, 0), axis=1)),
        ]
    )
    for stride in strides(groups):
        extents = jnp.maximum(
            extents,
            lax.ppermute(extents, "groups", [(g, g ^ stride) for g in range(groups)]),
        )
    mine = facts[:, 1] == me
    index = jnp.arange(requests)
    earlier = index[None, :] < index[:, None]
    packed_earlier = (near[:, None, :] < near[:, :, None]) | (
        (near[:, None, :] == near[:, :, None]) & earlier[None]
    )
    starts_all = jnp.sum(jnp.where(packed_earlier, sizes_all[:, None, :], 0), axis=2)
    rank = jnp.sum(jnp.where(earlier[None], mine[:, None, :].astype(jnp.int32), 0), axis=2)
    chosen = mine[:, None, :] & (rank[:, None, :] == jnp.arange(capacity)[None, :, None])

    def chosen_of(values):
        return jnp.sum(jnp.where(chosen, values, 0), axis=2).reshape(-1)

    plan = jnp.concatenate(
        [
            sources,
            chosen_of(starts_all[:, None, :]),
            jnp.where(remaining_device, chosen_of(sizes_all[:, None, :]), 0),
            chosen_of(index[None, None, :] + 1) - 1,
        ]
    )
    plan_shape = (instances, capacity)

    local_output = attend(own_keys, own_values, cache_length, queries, own_fresh_k, own_fresh_v)
    near_sizes = list(range(6 * step, (most - cut) * 11 // 16, step)) + [most - cut]
    far_sizes = near_sizes[-2:]
    rests, pool = prepare(rest, near_sizes, (1, 1, slot_count, 2, span_rows, group_width))
    local_output, pool, rests, extents, plan = lax.optimization_barrier(
        (local_output, pool, rests, extents, plan)
    )
    local_rows = local_output
    local_output = jnp.where(remaining_device, local_output, jnp.zeros_like(local_output))
    first, local_rows, local_output = lax.optimization_barrier((first, local_rows, local_output))

    def finish(more, far, rests, first, local_rows, plan, pool):
        piece = down(rests[near_sizes.index(more)])
        away = across(first, all_steps[0], 0)
        inherited = place(plan, *plan_shape, spread(local_rows, all_steps, halved_count))
        inherited = down(inherited)
        inherited = jnp.where(remaining_device, inherited, jnp.zeros_like(inherited))
        parts = [part + (0, cut) for part in spread(first, all_steps[1:])]
        pool = unpack(plan, *plan_shape, parts, pool)
        away, piece, pool, inherited = lax.optimization_barrier((away, piece, pool, inherited))
        parts = [
            (part, order.index(order[number] ^ all_steps[0]), 0, cut)
            for part, number in spread(away, all_steps[1:])
        ]
        pieces = [
            part + (cut, cut + more)
            for part in spread(piece, all_steps if far else all_steps[1:])
        ]
        pool = unpack(plan, *plan_shape, [parts[0], pieces[0]], pool)
        return inherited, unpack(plan, *plan_shape, parts[1:] + pieces[1:], pool)

    branches = [functools.partial(finish, more, False) for more in near_sizes]
    branches += [functools.partial(finish, more, True) for more in far_sizes]
    extra = jnp.maximum(extents[0] - cut, 0)
    near_choice = sum((extra > size).astype(jnp.int32) for size in near_sizes[:-1])
    far_choice = sum((extra > size).astype(jnp.int32) for size in far_sizes[:-1])
    choice = jnp.where(extents[1] > cut, len(near_sizes) + far_choice, near_choice)
    inherited, kept_cache = lax.switch(choice, branches, rests, first, local_rows, plan, pool)
    return (local_output, inherited[None, None], kept_cache)


def solution(mesh):
    placed = (
        P(("groups", "inst"), None, None),
        P(("groups", "inst"), None, "tp"),
        P(("groups", "inst"), None, "tp"),
        P(("groups", "inst"), None, "tp"),
        P(("groups", "inst"), None),
        P(("groups", "inst")),
        P(("groups", "inst"), None),
        P(None, "tp"),
        P(None, "tp"),
    )
    return jax.shard_map(
        local,
        mesh=mesh,
        in_specs=placed,
        out_specs=(
            P(("groups", "inst"), None, "tp"),
            P(("groups", "inst"), "tp", None, None, None),
            P(("groups", "inst"), "tp", None, None, None, None),
        ),
        check_vma=False,
    )
```
